32 devices in a mesh: wide: 8 (over z, y), narrow: 4 (over x, core).
Axes of the slice: x: 2, y: 2, z: 4, core: 2. Of those that a mesh axis runs over, the one named last changes fastest.
Arguments:
- residual_in: bfloat16 [16, 7168], P('wide', 'narrow'), may hold values from -2 to 2
- query_nope: bfloat16 [16, 64, 128], P('wide', 'narrow'), may hold values from -6 to 6
- query_rope: bfloat16 [16, 64, 64], P('wide', 'narrow'), may hold values from -8 to 8
- absorb_key: bfloat16 [64, 128, 512], P('narrow'), may hold values from -0.5 to 0.5
- absorb_value: bfloat16 [64, 512, 128], P('narrow'), may hold values from -0.25 to 0.25
- latent_cache: bfloat16 [16, 2048, 576], P('wide'), may hold values from -8 to 8
- cache_lengths: int32 [16], P('wide'), may hold values from 256 to 2048, as said below
- slot_rows: int32 [16], replicated, may hold values from 0 to 15, each once
- out_proj: bfloat16 [8192, 7168], P('wide', 'narrow'), may hold values from -0.0625 to 0.0625
- norm_gain: bfloat16 [7168], P('narrow'), may hold values from 0.25 to 1.75
- gate_weight: bfloat16 [7168, 18432], P('narrow', 'wide'), may hold values from -0.0625 to 0.0625
- up_weight: bfloat16 [7168, 18432], P('narrow', 'wide'), may hold values from -0.0625 to 0.0625
- down_weight: bfloat16 [18432, 7168], P('wide', 'narrow'), may hold values from -0.046875 to 0.046875
Outputs:
- residual_out: bfloat16 [16, 7168], P('wide', 'narrow')
The draws below stay inside these ranges and needn't reach their ends.
Inputs may be any that keep to these rules, and one draw needn't show every extreme that they name: `cache_lengths`: every slot has at least 256 live positions; in every draw some slot is full. `slot_rows`: each batch row is named by exactly one slot.
All inputs are finite; a program needn't handle non-finite values.
Results may differ from the reference program's by a relative error of at most 0.009.
Values may be sent and summed in bfloat16 or wider, within the bound.
No kernel may reach another device: no remote copies, remote signals or barrier semaphores. Data moves between devices by JAX's collectives and lax.ppermute only.
A program may use at most 64 MiB of HBM per device.

```python
import math
import jax
import jax.numpy as jnp
from jax import lax

D = 7168
H = 64
HD = 128
LAT = 512
ROPE = 64
FF = 18432
LCAP = 2048
ROWS = 16


def draw_latent_cache(key, part):
    base_draw = jax.random.truncated_normal(jax.random.fold_in(key, 11), -6.0, 6.0, (ROWS, LCAP, LAT + ROPE), jnp.float32)
    return base_draw.astype(jnp.bfloat16)


def draw_query_rope(key, part):
    base_draw = jax.random.truncated_normal(jax.random.fold_in(key, 13), -6.0, 6.0, (ROWS, H, ROPE), jnp.float32)
    return base_draw.astype(jnp.bfloat16)


def draw_cache_lengths(key, part):
    drawn = jax.random.randint(jax.random.fold_in(key, 17), (ROWS,), LCAP // 8, LCAP + 1, dtype=jnp.int32)
    full_slot = jax.random.randint(jax.random.fold_in(key, 19), (), 0, ROWS, dtype=jnp.int32)
    return jnp.where(jnp.arange(ROWS, dtype=jnp.int32) == full_slot, LCAP, drawn).astype(jnp.int32)


def levels(own_key, dims, pieces, low, largest):
    def one(position, parts):
        steps = jax.random.uniform(jax.random.fold_in(jax.random.fold_in(own_key, 6), position), (parts,), jnp.float32, low / len(pieces), largest / len(pieces))
        return jnp.repeat(jnp.exp(steps), dims[position] // parts).reshape((-1,) + (1,) * (len(dims) - position - 1))

    loudness = one(*pieces[0])
    for cut in pieces[1:]:
        loudness = loudness * one(*cut)
    return loudness


def noise(own_key, shape, scale, reach, split=(), kind=jnp.bfloat16):
    gain = levels(own_key, shape, split, -0.22, 0.18) if split else 1.0
    values = jax.random.normal(own_key, shape, jnp.float32) * scale * gain
    return jnp.minimum(jnp.maximum(values, -reach), reach).astype(kind)


def setup_inputs(seed: int = 0) -> dict:
    key_list = jax.random.split(jax.random.key(seed), 14)
    return {
        "residual_in": noise(key_list[0], (ROWS, D), 0.3, 2.0, ((0, 8), (1, 4))),
        "query_nope": noise(key_list[1], (ROWS, H, HD), 1.0, 6.0, ((0, 8), (1, 4))),
        "query_rope": draw_query_rope(jax.random.fold_in(key_list[13], 71), 0),
        "absorb_key": noise(key_list[3], (H, HD, LAT), HD ** -0.5, 0.5, ((0, 4),)),
        "absorb_value": noise(key_list[4], (H, LAT, HD), LAT ** -0.5, 0.25, ((0, 4),)),
        "latent_cache": draw_latent_cache(jax.random.fold_in(key_list[13], 71), 0),
        "cache_lengths": draw_cache_lengths(jax.random.fold_in(key_list[13], 71), 0),
        "slot_rows": jax.random.permutation(key_list[7], ROWS).astype(jnp.int32),
        "out_proj": noise(key_list[8], (H * HD, D), (H * HD) ** -0.5, 0.0625, ((0, 8), (1, 4))),
        "norm_gain": jnp.clip(1.0 + 0.15 * jax.random.normal(key_list[9], (D,), jnp.float32), 0.25, 1.75).astype(jnp.bfloat16),
        "gate_weight": noise(key_list[10], (D, FF), D ** -0.5, 0.0625, ((0, 4), (1, 8))),
        "up_weight": noise(key_list[11], (D, FF), D ** -0.5, 0.0625, ((0, 4), (1, 8))),
        "down_weight": noise(key_list[12], (FF, D), FF ** -0.5, 0.046875, ((0, 8), (1, 4))),
    }


def reference(residual_in, query_nope, query_rope, absorb_key, absorb_value, latent_cache, cache_lengths, slot_rows, out_proj, norm_gain, gate_weight, up_weight, down_weight):
    query_latent = jnp.einsum('bhd,hdc->bhc', query_nope.astype(jnp.float32), absorb_key.astype(jnp.float32)).astype(jnp.bfloat16)
    queries = jnp.take(jnp.concatenate([query_latent, query_rope], axis=2), slot_rows, axis=0)
    scale = 1.0 / math.sqrt(HD + ROPE)
    positions = jnp.arange(LCAP, dtype=jnp.int32)

    def one_slot(packed):
        query_slot, cache_slot, length = packed
        scores = jnp.dot(query_slot, cache_slot.T, preferred_element_type=jnp.float32) * scale
        live = positions[None, :] < length
        scores = jnp.where(live, scores, -jnp.inf)
        highest = lax.optimization_barrier(jnp.max(scores, axis=1, keepdims=True))
        weights = jnp.where(live, jnp.exp(scores - highest), 0.0)
        probs = (weights / lax.optimization_barrier(jnp.sum(weights, axis=1, keepdims=True))).astype(jnp.bfloat16)
        context = jnp.dot(probs, cache_slot, preferred_element_type=jnp.float32)
        return context[:, :LAT].astype(jnp.bfloat16)
    context = lax.map(one_slot, (queries, latent_cache, cache_lengths))
    heads_out = jnp.einsum('shc,hcd->shd', context.astype(jnp.float32), absorb_value.astype(jnp.float32)).astype(jnp.bfloat16)
    heads_out = heads_out.reshape(ROWS, H * HD)
    slot_attn = jnp.dot(heads_out, out_proj, preferred_element_type=jnp.float32)
    attention = jnp.take(slot_attn, jnp.argsort(slot_rows), axis=0)
    middle = residual_in.astype(jnp.float32) + attention
    mean_square = lax.optimization_barrier(jnp.mean(middle * middle, axis=1, keepdims=True))
    normed = (middle * lax.rsqrt(mean_square + 1e-06) * norm_gain.astype(jnp.float32)).astype(jnp.bfloat16)
    gate = jnp.dot(normed, gate_weight, preferred_element_type=jnp.float32)
    upward = jnp.dot(normed, up_weight, preferred_element_type=jnp.float32)
    hidden = (jax.nn.silu(gate) * upward).astype(jnp.bfloat16)
    return (middle + jnp.dot(hidden, down_weight, preferred_element_type=jnp.float32)).astype(jnp.bfloat16)
```

```python
import functools
import math

import jax
import jax.numpy as jnp
from jax import lax
from jax.experimental import pallas as pl
from jax.experimental.pallas import tpu as pltpu
from jax.sharding import PartitionSpec as P

D = 7168
BF16 = jnp.bfloat16
F32 = jnp.float32
VMEM = pl.BlockSpec(memory_space=pltpu.VMEM)
SMEM = pl.BlockSpec(memory_space=pltpu.SMEM)
NT = (((1,), (1,)), ((), ()))


def near(array):
    return pltpu.with_memory_space_constraint(array, pltpu.VMEM)


def call(kernel, out_shape, in_specs, name):
    return pl.pallas_call(
        kernel,
        out_shape=out_shape,
        in_specs=in_specs,
        out_specs=jax.tree.map(lambda _: VMEM, out_shape),
        compiler_params=pltpu.CompilerParams(vmem_limit_bytes=16 * 1024 * 1024),
        name=name,
    )


def attend_kernel(
    narrow, blocks, scale, rows_ref, lengths_ref, query_ref, key_ref, cache_ref, value_ref, out_ref
):
    slots, latent = cache_ref.shape[0], value_ref.shape[1]
    heads, head_size = key_ref.shape[0], key_ref.shape[1]
    rope = cache_ref.shape[1] - latent
    span = cache_ref.shape[2]
    queries = []
    for slot in range(slots):
        row = rows_ref[slot]
        queries.append(query_ref[row // slots, row % slots])
    query = jnp.concatenate(queries, axis=0)
    own_head = lax.broadcasted_iota(jnp.int32, (slots * heads, 1), 0) % heads
    nope = query[:, :head_size]
    zero = jnp.zeros((), BF16)
    spread = jnp.concatenate(
        [jnp.where(own_head == head, nope, zero) for head in range(heads)], axis=1
    )
    query_latent = jnp.dot(
        spread, key_ref[...].reshape(heads * head_size, latent), preferred_element_type=F32
    ).astype(BF16)
    contexts = []
    for slot in range(slots):
        part = slice(slot * heads, (slot + 1) * heads)
        scores = jnp.dot(
            query_latent[part], cache_ref[slot, :latent, :], preferred_element_type=F32
        ) + jnp.dot(
            query[part, head_size : head_size + rope],
            cache_ref[slot, latent:, :],
            preferred_element_type=F32,
        )
        live = lax.broadcasted_iota(jnp.int32, (1, span), 1) < lengths_ref[slot]
        scores = jnp.where(live, scores * scale, -jnp.inf)
        weights = jnp.exp(scores - jnp.max(scores, axis=1, keepdims=True))
        probs = (weights / jnp.sum(weights, axis=1, keepdims=True)).astype(BF16)
        contexts.append(
            lax.dot_general(
                probs, cache_ref[slot, :latent, :], NT, preferred_element_type=F32
            ).astype(BF16)
        )
    context = jnp.concatenate(contexts, axis=0)
    spread = jnp.concatenate(
        [jnp.where(own_head == head, context, zero) for head in range(heads)], axis=1
    )
    heads_out = jnp.dot(
        spread, value_ref[...].reshape(heads * latent, head_size), preferred_element_type=F32
    ).astype(BF16)
    per_block = heads // blocks
    pieces = []
    for block in range(blocks):
        low = block * per_block
        pieces.append(
            jnp.concatenate(
                [
                    heads_out[slot * heads + low : slot * heads + low + per_block]
                    for slot in range(slots)
                ],
                axis=0,
            )
        )
    for target in range(out_ref.shape[0]):
        out_ref[target] = pieces[(target // narrow) % blocks]


def project_kernel(narrow, blocks, rows_ref, group_ref, heads_ref, residual_ref, weight_ref, out_ref):
    wide = heads_ref.shape[0] // narrow
    slots = residual_ref.shape[0]
    rows = wide * slots
    per_block = heads_ref.shape[1] // slots
    head_size = heads_ref.shape[2]
    group = group_ref[0]
    holder = group // blocks
    received = jnp.concatenate(
        [heads_ref[source * narrow + holder] for source in range(wide)], axis=0
    )
    count = rows * per_block
    column = lax.broadcasted_iota(jnp.int32, (1, count), 1)
    column_row = jnp.zeros((1, count), jnp.int32)
    for slot in range(rows):
        column_row = jnp.where(column // per_block == slot, rows_ref[slot], column_row)
    wanted = column_row + rows * (column % per_block)
    position = lax.broadcasted_iota(jnp.int32, (count, count), 0)
    select = jnp.where(position == wanted, 1.0, 0.0).astype(BF16)
    ordered = jnp.dot(select, received, preferred_element_type=F32).astype(BF16)
    flat = jnp.concatenate(
        [ordered[head * rows : (head + 1) * rows] for head in range(per_block)], axis=1
    )
    total = jnp.dot(flat, weight_ref[...], preferred_element_type=F32)
    row = lax.broadcasted_iota(jnp.int32, (rows, 1), 0)
    for slot in range(slots):
        own = residual_ref[slot : slot + 1, :].astype(F32)
        total = total + jnp.where(row == group * slots + slot, own, 0.0)
    out_ref[...] = total.astype(BF16)


def split_sum(value):
    high = value.astype(BF16)
    low = (value - high.astype(F32)).astype(BF16)
    return high, low


def put_sums(out_ref, start, value):
    high, low = split_sum(value)
    shape = (value.shape[0], 128)
    out_ref[:, start : start + 128] = jnp.broadcast_to(high, shape)
    out_ref[:, start + 128 : start + 256] = jnp.broadcast_to(low, shape)


def get_sums(ref, start):
    return ref[:, start : start + 1].astype(F32) + ref[:, start + 128 : start + 129].astype(F32)


def expand_kernel(first_ref, second_ref, gain_ref, gate_ref, up_ref, middle_ref, out_ref):
    middle = first_ref[...].astype(F32) + second_ref[...].astype(F32)
    middle_ref[...] = middle
    columns = gate_ref.shape[1]
    padded = (out_ref.shape[1] - 256) // 2
    scaled = (middle * gain_ref[...].astype(F32)).astype(BF16)
    out_ref[:, :columns] = jnp.dot(scaled, gate_ref[...], preferred_element_type=F32).astype(BF16)
    out_ref[:, padded : padded + columns] = jnp.dot(
        scaled, up_ref[...], preferred_element_type=F32
    ).astype(BF16)
    put_sums(out_ref, 2 * padded, jnp.sum(middle * middle, axis=1, keepdims=True))


def merge_kernel(first_ref, second_ref, out_ref):
    end = out_ref.shape[1] - 256
    out_ref[:, :end] = (
        first_ref[:, :end].astype(F32) + second_ref[:, :end].astype(F32)
    ).astype(BF16)
    put_sums(out_ref, end, get_sums(first_ref, end) + get_sums(second_ref, end))


def contract_kernel(first_ref, second_ref, weight_ref, out_ref):
    padded = (first_ref.shape[1] - 256) // 2
    columns = weight_ref.shape[0]
    square = get_sums(first_ref, 2 * padded) + get_sums(second_ref, 2 * padded)
    factor = lax.rsqrt(square / D + 1e-06)
    gate = (first_ref[:, :columns].astype(F32) + second_ref[:, :columns].astype(F32)) * factor
    up = (
        first_ref[:, padded : padded + columns].astype(F32)
        + second_ref[:, padded : padded + columns].astype(F32)
    ) * factor
    hidden = (gate / (1.0 + jnp.exp(-gate)) * up).astype(BF16)
    total = jnp.dot(hidden, weight_ref[...], preferred_element_type=F32)
    slots = out_ref.shape[1]
    for owner in range(out_ref.shape[0]):
        out_ref[owner] = total[owner * slots : (owner + 1) * slots]


def swap(array, axis, distance, size):
    return lax.ppermute(array, axis, [(i, i ^ distance) for i in range(size)])


def shards(
    wide,
    narrow,
    residual_in,
    query_nope,
    query_rope,
    absorb_key,
    absorb_value,
    latent_cache,
    cache_lengths,
    slot_rows,
    out_proj,
    norm_gain,
    gate_weight,
    up_weight,
    down_weight,
):
    slots, heads, head_size = query_nope.shape
    rope = query_rope.shape[2]
    features = out_proj.shape[1]
    rows = slot_rows.shape[0]
    per_block = out_proj.shape[0] // head_size
    blocks = heads // per_block
    group = lax.axis_index("wide").astype(jnp.int32)
    scale = 1.0 / math.sqrt(head_size + rope)

    padding = jnp.zeros((slots, heads, 128 - rope), BF16)
    packed = jnp.concatenate([query_nope, query_rope, padding], axis=2)
    queries = lax.all_to_all(
        jnp.broadcast_to(packed[None], (wide,) + packed.shape), "wide", 0, 0, tiled=True
    )
    my_rows = lax.dynamic_slice_in_dim(slot_rows, group * slots, slots)
    heads_out = call(
        functools.partial(attend_kernel, narrow, blocks, scale),
        jax.ShapeDtypeStruct((wide * narrow, slots * per_block, head_size), BF16),
        [SMEM, SMEM, VMEM, VMEM, VMEM, VMEM],
        "attend",
    )(
        my_rows,
        cache_lengths,
        queries,
        near(absorb_key),
        near(jnp.swapaxes(latent_cache, 1, 2)),
        near(absorb_value),
    )
    received = lax.all_to_all(heads_out, ("wide", "narrow"), 0, 0, tiled=True)
    summed = call(
        functools.partial(project_kernel, narrow, blocks),
        jax.ShapeDtypeStruct((rows, features), BF16),
        [SMEM, SMEM, VMEM, VMEM, VMEM],
        "project",
    )(slot_rows, group[None], received, residual_in, near(out_proj))
    distance = 1
    while distance < wide:
        other = swap(summed, "wide", distance, wide)
        distance *= 2
        if distance < wide:
            summed = (summed.astype(F32) + other.astype(F32)).astype(BF16)
    columns = gate_weight.shape[1]
    padded = -(-columns // 128) * 128
    middle, terms = call(
        expand_kernel,
        (
            jax.ShapeDtypeStruct((rows, features), F32),
            jax.ShapeDtypeStruct((rows, 2 * padded + 256), BF16),
        ),
        [VMEM] * 5,
        "expand",
    )(summed, other, norm_gain[None, :], near(gate_weight), near(up_weight))
    distance = 1
    while distance < narrow:
        other = swap(terms, "narrow", distance, narrow)
        distance *= 2
        if distance < narrow:
            terms = call(merge_kernel, terms_like(terms), [VMEM] * 2, "merge")(terms, other)
    down = call(
        contract_kernel,
        jax.ShapeDtypeStruct((wide, slots, features), F32),
        [VMEM] * 3,
        "contract",
    )(terms, other, near(down_weight))
    total = jnp.sum(lax.all_to_all(down, "wide", 0, 0, tiled=True), axis=0)
    return (lax.dynamic_slice_in_dim(middle, group * slots, slots) + total).astype(BF16)


def terms_like(array):
    return jax.ShapeDtypeStruct(array.shape, array.dtype)


def solution(mesh):
    in_specs = (
        P("wide", "narrow"),
        P("wide", "narrow", None),
        P("wide", "narrow", None),
        P("narrow", None, None),
        P("narrow", None, None),
        P("wide", None, None),
        P("wide"),
        P(),
        P("wide", "narrow"),
        P("narrow"),
        P("narrow", "wide"),
        P("narrow", "wide"),
        P("wide", "narrow"),
    )
    out_specs = P("wide", "narrow")
    body = functools.partial(shards, mesh.shape["wide"], mesh.shape["narrow"])
    return jax.shard_map(body, mesh=mesh, in_specs=in_specs, out_specs=out_specs, check_vma=False)
```

```python
import functools
import math

import jax
import jax.numpy as jnp
from jax import lax
from jax.experimental import pallas as pl
from jax.experimental.pallas import tpu as pltpu
from jax.sharding import PartitionSpec as P

D = 7168
BF16 = jnp.bfloat16
F32 = jnp.float32
VMEM = pl.BlockSpec(memory_space=pltpu.VMEM)
SMEM = pl.BlockSpec(memory_space=pltpu.SMEM)
HBM = pl.BlockSpec(memory_space=pltpu.HBM)
NT = (((1,), (1,)), ((), ()))


def far(array):
    return pltpu.with_memory_space_constraint(array, pltpu.HBM)


def call(kernel, out_shape, in_specs, name, scratch=()):
    return pl.pallas_call(
        kernel,
        out_shape=out_shape,
        scratch_shapes=scratch,
        in_specs=in_specs,
        out_specs=jax.tree.map(lambda _: VMEM, out_shape),
        compiler_params=pltpu.CompilerParams(vmem_limit_bytes=16 * 1024 * 1024),
        name=name,
    )


def pack_kernel(nope_hbm, rope_hbm, out_ref, nope_ref, rope_ref, sems):
    copies = [
        pltpu.make_async_copy(nope_hbm, nope_ref, sems.at[0]),
        pltpu.make_async_copy(rope_hbm, rope_ref, sems.at[1]),
    ]
    for copy in copies:
        copy.start()
    head_size, width = nope_ref.shape[2], rope_ref.shape[2]
    empty = jnp.zeros(rope_ref.shape[:2] + (out_ref.shape[3] - head_size - width,), BF16)
    for copy in copies:
        copy.wait()
    row = jnp.concatenate([nope_ref[...], rope_ref[...], empty], axis=2)
    for target in range(out_ref.shape[0]):
        out_ref[target] = row


class Fetch:
    def __init__(self, source, target, sems, first, parts):
        self.copies = [
            pltpu.make_async_copy(source.at[part], target.at[part], sems.at[first + index])
            for index, part in enumerate(parts)
        ]

    def start(self):
        for copy in self.copies:
            copy.start()
        return self

    def wait(self, first=0, last=None):
        for copy in self.copies[first:last]:
            copy.wait()


def halves(size):
    if size % 32:
        return [pl.ds(0, size)]
    return [pl.ds(0, size // 2), pl.ds(size // 2, size // 2)]


def attend_kernel(
    narrow,
    blocks,
    scale,
    group_ref,
    rows_hbm,
    lengths_hbm,
    query_ref,
    key_hbm,
    cache_hbm,
    value_hbm,
    weight_hbm,
    out_ref,
    weight_ref,
    rows_ref,
    lengths_ref,
    key_ref,
    cache_ref,
    value_ref,
    sems,
):
    slots, latent = cache_ref.shape[0], value_ref.shape[1]
    heads, head_size = key_ref.shape[0], key_ref.shape[1]
    rope = cache_ref.shape[1] - latent
    span = cache_ref.shape[2]
    small = [
        pltpu.make_async_copy(rows_hbm, rows_ref, sems.at[0]),
        pltpu.make_async_copy(lengths_hbm, lengths_ref, sems.at[1]),
    ]
    for copy in small:
        copy.start()
    key = Fetch(key_hbm, key_ref, sems, 2, [pl.ds(0, heads // 2), pl.ds(heads // 2, heads // 2)]).start()
    wide_cut = [(slot, part) for slot in range(slots) for part in halves(cache_ref.shape[1])]
    cache = Fetch(cache_hbm, cache_ref, sems, 4, wide_cut).start()
    value = Fetch(
        value_hbm, value_ref, sems, 4 + 2 * slots, [pl.ds(0, heads // 2), pl.ds(heads // 2, heads // 2)]
    ).start()
    weight = Fetch(
        weight_hbm, weight_ref, sems, 6 + 2 * slots, halves(weight_ref.shape[0])
    ).start()
    for copy in small:
        copy.wait()
    group = group_ref[0]
    queries = []
    for slot in range(slots):
        row = rows_ref[group * slots + slot]
        queries.append(query_ref[row // slots, row % slots])
    query = jnp.concatenate(queries, axis=0)
    own_head = lax.broadcasted_iota(jnp.int32, (slots * heads, 1), 0) % heads
    nope = query[:, :head_size]
    zero = jnp.zeros((), BF16)
    spread = jnp.concatenate(
        [jnp.where(own_head == head, nope, zero) for head in range(heads)], axis=1
    )
    key.wait()
    query_latent = jnp.dot(
        spread, key_ref[...].reshape(heads * head_size, latent), preferred_element_type=F32
    ).astype(BF16)
    contexts = []
    for slot in range(slots):
        part = slice(slot * heads, (slot + 1) * heads)
        per_slot = len(wide_cut) // slots
        cache.wait(slot * per_slot, (slot + 1) * per_slot)
        scores = jnp.dot(
            query_latent[part], cache_ref[slot, :latent, :], preferred_element_type=F32
        ) + jnp.dot(
            query[part, head_size : head_size + rope],
            cache_ref[slot, latent:, :],
            preferred_element_type=F32,
        )
        live = lax.broadcasted_iota(jnp.int32, (1, span), 1) < lengths_ref[slot]
        scores = jnp.where(live, scores * scale, -jnp.inf)
        weights = jnp.exp(scores - jnp.max(scores, axis=1, keepdims=True))
        probs = (weights / jnp.sum(weights, axis=1, keepdims=True)).astype(BF16)
        contexts.append(
            lax.dot_general(
                probs, cache_ref[slot, :latent, :], NT, preferred_element_type=F32
            ).astype(BF16)
        )
    context = jnp.concatenate(contexts, axis=0)
    spread = jnp.concatenate(
        [jnp.where(own_head == head, context, zero) for head in range(heads)], axis=1
    )
    value.wait()
    heads_out = jnp.dot(
        spread, value_ref[...].reshape(heads * latent, head_size), preferred_element_type=F32
    ).astype(BF16)
    per_block = heads // blocks
    pieces = []
    for block in range(blocks):
        low = block * per_block
        pieces.append(
            jnp.concatenate(
                [
                    heads_out[slot * heads + low : slot * heads + low + per_block]
                    for slot in range(slots)
                ],
                axis=0,
            )
        )
    for target in range(out_ref.shape[0]):
        out_ref[target] = pieces[(target // narrow) % blocks]
    weight.wait()


def project_kernel(narrow, blocks, rows_ref, group_ref, heads_ref, residual_ref, weight_ref, out_ref):
    wide = heads_ref.shape[0] // narrow
    slots = residual_ref.shape[0]
    rows = wide * slots
    per_block = heads_ref.shape[1] // slots
    head_size = heads_ref.shape[2]
    group = group_ref[0]
    holder = group // blocks
    received = jnp.concatenate(
        [heads_ref[source * narrow + holder] for source in range(wide)], axis=0
    )
    count = rows * per_block
    column = lax.broadcasted_iota(jnp.int32, (1, count), 1)
    column_row = jnp.zeros((1, count), jnp.int32)
    for slot in range(rows):
        column_row = jnp.where(column // per_block == slot, rows_ref[slot], column_row)
    wanted = column_row + rows * (column % per_block)
    position = lax.broadcasted_iota(jnp.int32, (count, count), 0)
    select = jnp.where(position == wanted, 1.0, 0.0).astype(BF16)
    ordered = jnp.dot(select, received, preferred_element_type=F32).astype(BF16)
    flat = jnp.concatenate(
        [ordered[head * rows : (head + 1) * rows] for head in range(per_block)], axis=1
    )
    total = jnp.dot(flat, weight_ref[...], preferred_element_type=F32)
    row = lax.broadcasted_iota(jnp.int32, (rows, 1), 0)
    for slot in range(slots):
        own = residual_ref[slot : slot + 1, :].astype(F32)
        total = total + jnp.where(row == group * slots + slot, own, 0.0)
    out_ref[...] = total.astype(BF16)


def split_sum(value):
    high = value.astype(BF16)
    low = (value - high.astype(F32)).astype(BF16)
    return high, low


def put_sums(out_ref, start, value):
    high, low = split_sum(value)
    shape = (value.shape[0], 128)
    out_ref[:, start : start + 128] = jnp.broadcast_to(high, shape)
    out_ref[:, start + 128 : start + 256] = jnp.broadcast_to(low, shape)


def get_sums(ref, start):
    return ref[:, start : start + 1].astype(F32) + ref[:, start + 128 : start + 129].astype(F32)


def expand_kernel(first_ref, second_ref, gain_ref, gate_ref, up_ref, middle_ref, out_ref):
    middle = first_ref[...].astype(F32) + second_ref[...].astype(F32)
    middle_ref[...] = middle
    columns = gate_ref.shape[1]
    padded = (out_ref.shape[1] - 256) // 2
    scaled = (middle * gain_ref[...].astype(F32)).astype(BF16)
    out_ref[:, :columns] = jnp.dot(scaled, gate_ref[...], preferred_element_type=F32).astype(BF16)
    out_ref[:, padded : padded + columns] = jnp.dot(
        scaled, up_ref[...], preferred_element_type=F32
    ).astype(BF16)
    put_sums(out_ref, 2 * padded, jnp.sum(middle * middle, axis=1, keepdims=True))


def merge_kernel(first_ref, second_ref, out_ref):
    end = out_ref.shape[1] - 256
    out_ref[:, :end] = (
        first_ref[:, :end].astype(F32) + second_ref[:, :end].astype(F32)
    ).astype(BF16)
    put_sums(out_ref, end, get_sums(first_ref, end) + get_sums(second_ref, end))


def contract_kernel(first_ref, second_ref, weight_ref, out_ref):
    padded = (first_ref.shape[1] - 256) // 2
    columns = weight_ref.shape[0]
    square = get_sums(first_ref, 2 * padded) + get_sums(second_ref, 2 * padded)
    factor = lax.rsqrt(square / D + 1e-06)
    gate = (first_ref[:, :columns].astype(F32) + second_ref[:, :columns].astype(F32)) * factor
    up = (
        first_ref[:, padded : padded + columns].astype(F32)
        + second_ref[:, padded : padded + columns].astype(F32)
    ) * factor
    hidden = (gate / (1.0 + jnp.exp(-gate)) * up).astype(BF16)
    total = jnp.dot(hidden, weight_ref[...], preferred_element_type=F32)
    slots = out_ref.shape[1]
    for owner in range(out_ref.shape[0]):
        out_ref[owner] = total[owner * slots : (owner + 1) * slots]


def swap(array, axis, distance, size):
    return lax.ppermute(array, axis, [(i, i ^ distance) for i in range(size)])


def shards(
    wide,
    narrow,
    residual_in,
    query_nope,
    query_rope,
    absorb_key,
    absorb_value,
    latent_cache,
    cache_lengths,
    slot_rows,
    out_proj,
    norm_gain,
    gate_weight,
    up_weight,
    down_weight,
):
    slots, heads, head_size = query_nope.shape
    rope = query_rope.shape[2]
    features = out_proj.shape[1]
    rows = slot_rows.shape[0]
    per_block = out_proj.shape[0] // head_size
    blocks = heads // per_block
    group = lax.axis_index("wide").astype(jnp.int32)
    scale = 1.0 / math.sqrt(head_size + rope)

    packed = call(
        pack_kernel,
        pltpu.VMEM((wide, slots, heads, head_size + 128), BF16),
        [HBM] * 2,
        "pack",
        [
            pltpu.VMEM(query_nope.shape, BF16),
            pltpu.VMEM(query_rope.shape, BF16),
            pltpu.SemaphoreType.DMA((2,)),
        ],
    )(far(query_nope), far(query_rope))
    queries = lax.all_to_all(packed, "wide", 0, 0, tiled=True)
    cache = jnp.swapaxes(latent_cache, 1, 2)
    heads_out, out_weight = call(
        functools.partial(attend_kernel, narrow, blocks, scale),
        (
            pltpu.VMEM((wide * narrow, slots * per_block, head_size), BF16),
            pltpu.VMEM(out_proj.shape, BF16),
        ),
        [SMEM, HBM, HBM, VMEM, HBM, HBM, HBM, HBM],
        "attend",
        [
            pltpu.SMEM(slot_rows.shape, jnp.int32),
            pltpu.SMEM(cache_lengths.shape, jnp.int32),
            pltpu.VMEM(absorb_key.shape, BF16),
            pltpu.VMEM(cache.shape, BF16),
            pltpu.VMEM(absorb_value.shape, BF16),
            pltpu.SemaphoreType.DMA((8 + 2 * slots,)),
        ],
    )(
        group[None],
        far(slot_rows),
        far(cache_lengths),
        queries,
        far(absorb_key),
        far(cache),
        far(absorb_value),
        far(out_proj),
    )
    received = lax.all_to_all(heads_out, ("wide", "narrow"), 0, 0, tiled=True)
    summed = call(
        functools.partial(project_kernel, narrow, blocks),
        pltpu.VMEM((rows, features), BF16),
        [SMEM, SMEM, VMEM, VMEM, VMEM],
        "project",
    )(slot_rows, group[None], received, residual_in, out_weight)
    distance = 1
    while distance < wide:
        other = swap(summed, "wide", distance, wide)
        distance *= 2
        if distance < wide:
            summed = (summed.astype(F32) + other.astype(F32)).astype(BF16)
    columns = gate_weight.shape[1]
    padded = -(-columns // 128) * 128
    middle, terms = call(
        expand_kernel,
        (
            pltpu.VMEM((rows, features), F32),
            pltpu.VMEM((rows, 2 * padded + 256), BF16),
        ),
        [VMEM] * 5,
        "expand",
    )(summed, other, norm_gain[None, :], gate_weight, up_weight)
    distance = 1
    while distance < narrow:
        other = swap(terms, "narrow", distance, narrow)
        distance *= 2
        if distance < narrow:
            terms = call(merge_kernel, terms_like(terms), [VMEM] * 2, "merge")(terms, other)
    down = call(
        contract_kernel,
        pltpu.VMEM((wide, slots, features), F32),
        [VMEM] * 3,
        "contract",
    )(terms, other, down_weight)
    total = jnp.sum(lax.all_to_all(down, "wide", 0, 0, tiled=True), axis=0)
    return (lax.dynamic_slice_in_dim(middle, group * slots, slots) + total).astype(BF16)


def terms_like(array):
    return pltpu.VMEM(array.shape, array.dtype)


def solution(mesh):
    in_specs = (
        P("wide", "narrow"),
        P("wide", "narrow", None),
        P("wide", "narrow", None),
        P("narrow", None, None),
        P("narrow", None, None),
        P("wide", None, None),
        P("wide"),
        P(),
        P("wide", "narrow"),
        P("narrow"),
        P("narrow", "wide"),
        P("narrow", "wide"),
        P("wide", "narrow"),
    )
    out_specs = P("wide", "narrow")
    body = functools.partial(shards, mesh.shape["wide"], mesh.shape["narrow"])
    return jax.shard_map(body, mesh=mesh, in_specs=in_specs, out_specs=out_specs, check_vma=False)
```

```python
import functools
import math

import jax
import jax.numpy as jnp
from jax import lax
from jax.experimental import pallas as pl
from jax.experimental.pallas import tpu as pltpu
from jax.sharding import PartitionSpec as P

D = 7168
BF16 = jnp.bfloat16
F32 = jnp.float32
VMEM = pl.BlockSpec(memory_space=pltpu.VMEM)
SMEM = pl.BlockSpec(memory_space=pltpu.SMEM)
HBM = pl.BlockSpec(memory_space=pltpu.HBM)
NT = (((1,), (1,)), ((), ()))


def far(array):
    return pltpu.with_memory_space_constraint(array, pltpu.HBM)


def call(kernel, out_shape, in_specs, name, scratch=()):
    return pl.pallas_call(
        kernel,
        out_shape=out_shape,
        scratch_shapes=scratch,
        in_specs=in_specs,
        out_specs=jax.tree.map(lambda _: VMEM, out_shape),
        compiler_params=pltpu.CompilerParams(vmem_limit_bytes=16 * 1024 * 1024),
        name=name,
    )


def pack_kernel(group_ref, nope_hbm, rope_hbm, out_ref, nope_ref, rope_ref, sems):
    copies = [
        pltpu.make_async_copy(nope_hbm, nope_ref, sems.at[0]),
        pltpu.make_async_copy(rope_hbm, rope_ref, sems.at[1]),
    ]
    for copy in copies:
        copy.start()
    head_size, width = nope_ref.shape[2], rope_ref.shape[2]
    empty = jnp.zeros(rope_ref.shape[:2] + (out_ref.shape[3] - head_size - width,), BF16)
    for copy in copies:
        copy.wait()
    row = jnp.concatenate([nope_ref[...], rope_ref[...], empty], axis=2)
    for target in range(out_ref.shape[0]):
        out_ref[target] = row


class Fetch:
    def __init__(self, source, target, sems, first, parts):
        self.copies = [
            pltpu.make_async_copy(source.at[part], target.at[part], sems.at[first + index])
            for index, part in enumerate(parts)
        ]

    def start(self):
        for copy in self.copies:
            copy.start()
        return self

    def wait(self, first=0, last=None):
        for copy in self.copies[first:last]:
            copy.wait()


def halves(size):
    if size % 32:
        return [pl.ds(0, size)]
    return [pl.ds(0, size // 2), pl.ds(size // 2, size // 2)]


def attend_kernel(
    narrow,
    blocks,
    scale,
    group_ref,
    rows_hbm,
    lengths_hbm,
    query_ref,
    key_hbm,
    cache_hbm,
    value_hbm,
    weight_hbm,
    out_ref,
    weight_ref,
    rows_ref,
    lengths_ref,
    key_ref,
    cache_ref,
    value_ref,
    sems,
):
    slots, latent = cache_ref.shape[0], value_ref.shape[1]
    heads, head_size = key_ref.shape[0], key_ref.shape[1]
    rope = cache_ref.shape[1] - latent
    span = cache_ref.shape[2]
    small = [
        pltpu.make_async_copy(rows_hbm, rows_ref, sems.at[0]),
        pltpu.make_async_copy(lengths_hbm, lengths_ref, sems.at[1]),
    ]
    for copy in small:
        copy.start()
    key = Fetch(key_hbm, key_ref, sems, 2, [pl.ds(0, heads // 2), pl.ds(heads // 2, heads // 2)]).start()
    wide_cut = [(slot, part) for slot in range(slots) for part in halves(cache_ref.shape[1])]
    cache = Fetch(cache_hbm, cache_ref, sems, 4, wide_cut).start()
    value = Fetch(
        value_hbm, value_ref, sems, 4 + 2 * slots, [pl.ds(0, heads // 2), pl.ds(heads // 2, heads // 2)]
    ).start()
    weight = Fetch(
        weight_hbm, weight_ref, sems, 6 + 2 * slots, halves(weight_ref.shape[0])
    ).start()
    for copy in small:
        copy.wait()
    group = group_ref[0]
    queries = []
    for slot in range(slots):
        row = rows_ref[group * slots + slot]
        queries.append(query_ref[row // slots, row % slots])
    query = jnp.concatenate(queries, axis=0)
    own_head = lax.broadcasted_iota(jnp.int32, (slots * heads, 1), 0) % heads
    nope = query[:, :head_size]
    zero = jnp.zeros((), BF16)
    spread = jnp.concatenate(
        [jnp.where(own_head == head, nope, zero) for head in range(heads)], axis=1
    )
    key.wait()
    query_latent = jnp.dot(
        spread, key_ref[...].reshape(heads * head_size, latent), preferred_element_type=F32
    ).astype(BF16)
    contexts = []
    for slot in range(slots):
        part = slice(slot * heads, (slot + 1) * heads)
        per_slot = len(wide_cut) // slots
        cache.wait(slot * per_slot, (slot + 1) * per_slot)
        scores = jnp.dot(
            query_latent[part], cache_ref[slot, :latent, :], preferred_element_type=F32
        ) + jnp.dot(
            query[part, head_size : head_size + rope],
            cache_ref[slot, latent:, :],
            preferred_element_type=F32,
        )
        live = lax.broadcasted_iota(jnp.int32, (1, span), 1) < lengths_ref[slot]
        scores = jnp.where(live, scores * scale, -jnp.inf)
        weights = jnp.exp(scores - jnp.max(scores, axis=1, keepdims=True))
        probs = (weights / jnp.sum(weights, axis=1, keepdims=True)).astype(BF16)
        contexts.append(
            lax.dot_general(
                probs, cache_ref[slot, :latent, :], NT, preferred_element_type=F32
            ).astype(BF16)
        )
    context = jnp.concatenate(contexts, axis=0)
    spread = jnp.concatenate(
        [jnp.where(own_head == head, context, zero) for head in range(heads)], axis=1
    )
    value.wait()
    heads_out = jnp.dot(
        spread, value_ref[...].reshape(heads * latent, head_size), preferred_element_type=F32
    ).astype(BF16)
    per_block = heads // blocks
    pieces = []
    for block in range(blocks):
        low = block * per_block
        pieces.append(
            jnp.concatenate(
                [
                    heads_out[slot * heads + low : slot * heads + low + per_block]
                    for slot in range(slots)
                ],
                axis=0,
            )
        )
    for target in range(out_ref.shape[0]):
        out_ref[target] = pieces[(target // narrow) % blocks]
    weight.wait()


def project_kernel(narrow, blocks, rows_ref, group_ref, heads_ref, residual_ref, weight_ref, out_ref):
    wide = heads_ref.shape[0] // narrow
    slots = residual_ref.shape[0]
    rows = wide * slots
    per_block = heads_ref.shape[1] // slots
    head_size = heads_ref.shape[2]
    group = group_ref[0]
    holder = group // blocks
    received = jnp.concatenate(
        [heads_ref[source * narrow + holder] for source in range(wide)], axis=0
    )
    count = rows * per_block
    column = lax.broadcasted_iota(jnp.int32, (1, count), 1)
    column_row = jnp.zeros((1, count), jnp.int32)
    for slot in range(rows):
        column_row = jnp.where(column // per_block == slot, rows_ref[slot], column_row)
    wanted = column_row + rows * (column % per_block)
    position = lax.broadcasted_iota(jnp.int32, (count, count), 0)
    select = jnp.where(position == wanted, 1.0, 0.0).astype(BF16)
    ordered = jnp.dot(select, received, preferred_element_type=F32).astype(BF16)
    flat = jnp.concatenate(
        [ordered[head * rows : (head + 1) * rows] for head in range(per_block)], axis=1
    )
    total = jnp.dot(flat, weight_ref[...], preferred_element_type=F32)
    row = lax.broadcasted_iota(jnp.int32, (rows, 1), 0)
    for slot in range(slots):
        own = residual_ref[slot : slot + 1, :].astype(F32)
        total = total + jnp.where(row == group * slots + slot, own, 0.0)
    out_ref[...] = total.astype(BF16)


def split_sum(value):
    high = value.astype(BF16)
    low = (value - high.astype(F32)).astype(BF16)
    return high, low


def put_sums(out_ref, start, value):
    high, low = split_sum(value)
    shape = (value.shape[0], 128)
    out_ref[:, start : start + 128] = jnp.broadcast_to(high, shape)
    out_ref[:, start + 128 : start + 256] = jnp.broadcast_to(low, shape)


def get_sums(ref, start):
    return ref[:, start : start + 1].astype(F32) + ref[:, start + 128 : start + 129].astype(F32)


def expand_kernel(
    group_ref, first_ref, second_ref, gain_ref, gate_ref, up_ref, middle_ref, out_ref
):
    middle = first_ref[...].astype(F32) + second_ref[...].astype(F32)
    slots = middle_ref.shape[0]
    row = lax.broadcasted_iota(jnp.int32, (middle.shape[0], 1), 0)
    for slot in range(slots):
        own = jnp.where(row == group_ref[0] * slots + slot, middle, 0.0)
        middle_ref[slot : slot + 1] = jnp.sum(own, axis=0, keepdims=True)
    columns = gate_ref.shape[1]
    padded = (out_ref.shape[1] - 256) // 2
    scaled = (middle * gain_ref[...].astype(F32)).astype(BF16)
    out_ref[:, :columns] = jnp.dot(scaled, gate_ref[...], preferred_element_type=F32).astype(BF16)
    out_ref[:, padded : padded + columns] = jnp.dot(
        scaled, up_ref[...], preferred_element_type=F32
    ).astype(BF16)
    put_sums(out_ref, 2 * padded, jnp.sum(middle * middle, axis=1, keepdims=True))


def merge_kernel(first_ref, second_ref, out_ref):
    end = out_ref.shape[1] - 256
    out_ref[:, :end] = (
        first_ref[:, :end].astype(F32) + second_ref[:, :end].astype(F32)
    ).astype(BF16)
    put_sums(out_ref, end, get_sums(first_ref, end) + get_sums(second_ref, end))


def contract_kernel(first_ref, second_ref, weight_ref, out_ref):
    padded = (first_ref.shape[1] - 256) // 2
    columns = weight_ref.shape[0]
    square = get_sums(first_ref, 2 * padded) + get_sums(second_ref, 2 * padded)
    factor = lax.rsqrt(square / D + 1e-06)
    gate = (first_ref[:, :columns].astype(F32) + second_ref[:, :columns].astype(F32)) * factor
    up = (
        first_ref[:, padded : padded + columns].astype(F32)
        + second_ref[:, padded : padded + columns].astype(F32)
    ) * factor
    hidden = (gate / (1.0 + jnp.exp(-gate)) * up).astype(BF16)
    total = jnp.dot(hidden, weight_ref[...], preferred_element_type=F32)
    slots = out_ref.shape[1]
    for owner in range(out_ref.shape[0]):
        out_ref[owner] = total[owner * slots : (owner + 1) * slots]


def swap(array, axis, distance, size):
    return lax.ppermute(array, axis, [(i, i ^ distance) for i in range(size)])


def shards(
    wide,
    narrow,
    residual_in,
    query_nope,
    query_rope,
    absorb_key,
    absorb_value,
    latent_cache,
    cache_lengths,
    slot_rows,
    out_proj,
    norm_gain,
    gate_weight,
    up_weight,
    down_weight,
):
    slots, heads, head_size = query_nope.shape
    rope = query_rope.shape[2]
    features = out_proj.shape[1]
    rows = slot_rows.shape[0]
    per_block = out_proj.shape[0] // head_size
    blocks = heads // per_block
    group = lax.axis_index("wide").astype(jnp.int32)
    scale = 1.0 / math.sqrt(head_size + rope)

    packed = call(
        pack_kernel,
        pltpu.VMEM((wide, slots, heads, head_size + 128), BF16),
        [SMEM, HBM, HBM],
        "pack",
        [
            pltpu.VMEM(query_nope.shape, BF16),
            pltpu.VMEM(query_rope.shape, BF16),
            pltpu.SemaphoreType.DMA((2,)),
        ],
    )(group[None], far(query_nope), far(query_rope))
    queries = lax.all_to_all(packed, "wide", 0, 0, tiled=True)
    cache = jnp.swapaxes(latent_cache, 1, 2)
    heads_out, out_weight = call(
        functools.partial(attend_kernel, narrow, blocks, scale),
        (
            pltpu.VMEM((wide * narrow, slots * per_block, head_size), BF16),
            pltpu.VMEM(out_proj.shape, BF16),
        ),
        [SMEM, HBM, HBM, VMEM, HBM, HBM, HBM, HBM],
        "attend",
        [
            pltpu.SMEM(slot_rows.shape, jnp.int32),
            pltpu.SMEM(cache_lengths.shape, jnp.int32),
            pltpu.VMEM(absorb_key.shape, BF16),
            pltpu.VMEM(cache.shape, BF16),
            pltpu.VMEM(absorb_value.shape, BF16),
            pltpu.SemaphoreType.DMA((8 + 2 * slots,)),
        ],
    )(
        group[None],
        far(slot_rows),
        far(cache_lengths),
        queries,
        far(absorb_key),
        far(cache),
        far(absorb_value),
        far(out_proj),
    )
    received = lax.all_to_all(heads_out, ("wide", "narrow"), 0, 0, tiled=True)
    summed = call(
        functools.partial(project_kernel, narrow, blocks),
        pltpu.VMEM((rows, features), BF16),
        [SMEM, SMEM, VMEM, VMEM, VMEM],
        "project",
    )(slot_rows, group[None], received, residual_in, out_weight)
    distance = 1
    while distance < wide:
        other = swap(summed, "wide", distance, wide)
        distance *= 2
        if distance < wide:
            summed = (summed.astype(F32) + other.astype(F32)).astype(BF16)
    columns = gate_weight.shape[1]
    padded = -(-columns // 128) * 128
    middle, terms = call(
        expand_kernel,
        (
            pltpu.VMEM((slots, features), F32),
            pltpu.VMEM((rows, 2 * padded + 256), BF16),
        ),
        [SMEM] + [VMEM] * 5,
        "expand",
    )(group[None], summed, other, norm_gain[None, :], gate_weight, up_weight)
    distance = 1
    while distance < narrow:
        other = swap(terms, "narrow", distance, narrow)
        distance *= 2
        if distance < narrow:
            terms = call(merge_kernel, terms_like(terms), [VMEM] * 2, "merge")(terms, other)
    down = call(
        contract_kernel,
        pltpu.VMEM((wide, slots, features), F32),
        [VMEM] * 3,
        "contract",
    )(terms, other, down_weight)
    total = jnp.sum(lax.all_to_all(down, "wide", 0, 0, tiled=True), axis=0)
    return (middle + total).astype(BF16)


def terms_like(array):
    return pltpu.VMEM(array.shape, array.dtype)


def solution(mesh):
    in_specs = (
        P("wide", "narrow"),
        P("wide", "narrow", None),
        P("wide", "narrow", None),
        P("narrow", None, None),
        P("narrow", None, None),
        P("wide", None, None),
        P("wide"),
        P(),
        P("wide", "narrow"),
        P("narrow"),
        P("narrow", "wide"),
        P("narrow", "wide"),
        P("wide", "narrow"),
    )
    out_specs = P("wide", "narrow")
    body = functools.partial(shards, mesh.shape["wide"], mesh.shape["narrow"])
    return jax.shard_map(body, mesh=mesh, in_specs=in_specs, out_specs=out_specs, check_vma=False)
```

```python
import functools
import math

import jax
import jax.numpy as jnp
from jax import lax
from jax.experimental import pallas as pl
from jax.experimental.pallas import tpu as pltpu
from jax.sharding import PartitionSpec as P

D = 7168
BF16 = jnp.bfloat16
F32 = jnp.float32
VMEM = pl.BlockSpec(memory_space=pltpu.VMEM)
SMEM = pl.BlockSpec(memory_space=pltpu.SMEM)
HBM = pl.BlockSpec(memory_space=pltpu.HBM)
NT = (((1,), (1,)), ((), ()))


PACK = 10 * 10**9
ATTEND = 15 * 10**9
PROJECT = 12 * 10**9
EXPAND = 4 * 10**9
MERGE = 4 * 10**9
CONTRACT = 4 * 10**9


def near(array):
    return pltpu.with_memory_space_constraint(array, pltpu.VMEM)


def far(array):
    return pltpu.with_memory_space_constraint(array, pltpu.HBM)


def call(kernel, out_shape, in_specs, name, scratch=(), flops=0):
    return pl.pallas_call(
        kernel,
        out_shape=out_shape,
        scratch_shapes=scratch,
        cost_estimate=pl.CostEstimate(flops=flops, transcendentals=0, bytes_accessed=0),
        in_specs=in_specs,
        out_specs=jax.tree.map(lambda _: VMEM, out_shape),
        compiler_params=pltpu.CompilerParams(vmem_limit_bytes=16 * 1024 * 1024),
        name=name,
    )


def pack_kernel(group_ref, nope_hbm, rope_hbm, out_ref, nope_ref, rope_ref, sems):
    copies = [
        pltpu.make_async_copy(nope_hbm, nope_ref, sems.at[0]),
        pltpu.make_async_copy(rope_hbm, rope_ref, sems.at[1]),
    ]
    for copy in copies:
        copy.start()
    head_size, width = nope_ref.shape[2], rope_ref.shape[2]
    empty = jnp.zeros(rope_ref.shape[:2] + (out_ref.shape[3] - head_size - width,), BF16)
    for copy in copies:
        copy.wait()
    row = jnp.concatenate([nope_ref[...], rope_ref[...], empty], axis=2)
    for target in range(out_ref.shape[0]):
        out_ref[target] = row


def attend_kernel(
    narrow,
    blocks,
    scale,
    group_ref,
    rows_ref,
    lengths_ref,
    query_ref,
    key_ref,
    cache_ref,
    value_ref,
    out_ref,
):
    slots, latent = cache_ref.shape[0], value_ref.shape[1]
    heads, head_size = key_ref.shape[0], key_ref.shape[1]
    rope = cache_ref.shape[1] - latent
    span = cache_ref.shape[2]
    group = group_ref[0]
    queries = []
    for slot in range(slots):
        row = rows_ref[group * slots + slot]
        queries.append(query_ref[row // slots, row % slots])
    query = jnp.concatenate(queries, axis=0)
    own_head = lax.broadcasted_iota(jnp.int32, (slots * heads, 1), 0) % heads
    nope = query[:, :head_size]
    zero = jnp.zeros((), BF16)
    spread = jnp.concatenate(
        [jnp.where(own_head == head, nope, zero) for head in range(heads)], axis=1
    )
    query_latent = jnp.dot(
        spread, key_ref[...].reshape(heads * head_size, latent), preferred_element_type=F32
    ).astype(BF16)
    contexts = []
    for slot in range(slots):
        part = slice(slot * heads, (slot + 1) * heads)
        scores = jnp.dot(
            query_latent[part], cache_ref[slot, :latent, :], preferred_element_type=F32
        ) + jnp.dot(
            query[part, head_size : head_size + rope],
            cache_ref[slot, latent:, :],
            preferred_element_type=F32,
        )
        live = lax.broadcasted_iota(jnp.int32, (1, span), 1) < lengths_ref[slot]
        scores = jnp.where(live, scores * scale, -jnp.inf)
        weights = jnp.exp(scores - jnp.max(scores, axis=1, keepdims=True))
        probs = (weights / jnp.sum(weights, axis=1, keepdims=True)).astype(BF16)
        contexts.append(
            lax.dot_general(
                probs, cache_ref[slot, :latent, :], NT, preferred_element_type=F32
            ).astype(BF16)
        )
    context = jnp.concatenate(contexts, axis=0)
    spread = jnp.concatenate(
        [jnp.where(own_head == head, context, zero) for head in range(heads)], axis=1
    )
    heads_out = jnp.dot(
        spread, value_ref[...].reshape(heads * latent, head_size), preferred_element_type=F32
    ).astype(BF16)
    per_block = heads // blocks
    pieces = []
    for block in range(blocks):
        low = block * per_block
        pieces.append(
            jnp.concatenate(
                [
                    heads_out[slot * heads + low : slot * heads + low + per_block]
                    for slot in range(slots)
                ],
                axis=0,
            )
        )
    for target in range(out_ref.shape[0]):
        out_ref[target] = pieces[(target // narrow) % blocks]


def project_kernel(narrow, blocks, rows_ref, group_ref, heads_ref, residual_ref, weight_ref, out_ref):
    wide = heads_ref.shape[0] // narrow
    slots = residual_ref.shape[0]
    rows = wide * slots
    per_block = heads_ref.shape[1] // slots
    head_size = heads_ref.shape[2]
    group = group_ref[0]
    holder = group // blocks
    received = jnp.concatenate(
        [heads_ref[source * narrow + holder] for source in range(wide)], axis=0
    )
    count = rows * per_block
    column = lax.broadcasted_iota(jnp.int32, (1, count), 1)
    column_row = jnp.zeros((1, count), jnp.int32)
    for slot in range(rows):
        column_row = jnp.where(column // per_block == slot, rows_ref[slot], column_row)
    wanted = column_row + rows * (column % per_block)
    position = lax.broadcasted_iota(jnp.int32, (count, count), 0)
    select = jnp.where(position == wanted, 1.0, 0.0).astype(BF16)
    ordered = jnp.dot(select, received, preferred_element_type=F32).astype(BF16)
    flat = jnp.concatenate(
        [ordered[head * rows : (head + 1) * rows] for head in range(per_block)], axis=1
    )
    total = jnp.dot(flat, weight_ref[...], preferred_element_type=F32)
    row = lax.broadcasted_iota(jnp.int32, (rows, 1), 0)
    for slot in range(slots):
        own = residual_ref[slot : slot + 1, :].astype(F32)
        total = total + jnp.where(row == group * slots + slot, own, 0.0)
    out_ref[...] = total.astype(BF16)


def split_sum(value):
    high = value.astype(BF16)
    low = (value - high.astype(F32)).astype(BF16)
    return high, low


def put_sums(out_ref, start, value):
    high, low = split_sum(value)
    shape = (value.shape[0], 128)
    out_ref[:, start : start + 128] = jnp.broadcast_to(high, shape)
    out_ref[:, start + 128 : start + 256] = jnp.broadcast_to(low, shape)


def get_sums(ref, start):
    return ref[:, start : start + 1].astype(F32) + ref[:, start + 128 : start + 129].astype(F32)


def expand_kernel(
    group_ref, first_ref, second_ref, gain_ref, gate_ref, up_ref, middle_ref, out_ref
):
    middle = first_ref[...].astype(F32) + second_ref[...].astype(F32)
    slots = middle_ref.shape[0]
    row = lax.broadcasted_iota(jnp.int32, (middle.shape[0], 1), 0)
    for slot in range(slots):
        own = jnp.where(row == group_ref[0] * slots + slot, middle, 0.0)
        middle_ref[slot : slot + 1] = jnp.sum(own, axis=0, keepdims=True)
    columns = gate_ref.shape[1]
    padded = (out_ref.shape[1] - 256) // 2
    scaled = (middle * gain_ref[...].astype(F32)).astype(BF16)
    out_ref[:, :columns] = jnp.dot(scaled, gate_ref[...], preferred_element_type=F32).astype(BF16)
    out_ref[:, padded : padded + columns] = jnp.dot(
        scaled, up_ref[...], preferred_element_type=F32
    ).astype(BF16)
    put_sums(out_ref, 2 * padded, jnp.sum(middle * middle, axis=1, keepdims=True))


def merge_kernel(first_ref, second_ref, out_ref):
    end = out_ref.shape[1] - 256
    out_ref[:, :end] = (
        first_ref[:, :end].astype(F32) + second_ref[:, :end].astype(F32)
    ).astype(BF16)
    put_sums(out_ref, end, get_sums(first_ref, end) + get_sums(second_ref, end))


def contract_kernel(first_ref, second_ref, weight_ref, out_ref):
    padded = (first_ref.shape[1] - 256) // 2
    columns = weight_ref.shape[0]
    square = get_sums(first_ref, 2 * padded) + get_sums(second_ref, 2 * padded)
    factor = lax.rsqrt(square / D + 1e-06)
    gate = (first_ref[:, :columns].astype(F32) + second_ref[:, :columns].astype(F32)) * factor
    up = (
        first_ref[:, padded : padded + columns].astype(F32)
        + second_ref[:, padded : padded + columns].astype(F32)
    ) * factor
    hidden = (gate / (1.0 + jnp.exp(-gate)) * up).astype(BF16)
    total = jnp.dot(hidden, weight_ref[...], preferred_element_type=F32)
    slots = out_ref.shape[1]
    for owner in range(out_ref.shape[0]):
        out_ref[owner] = total[owner * slots : (owner + 1) * slots]


def swap(array, axis, distance, size):
    return lax.ppermute(array, axis, [(i, i ^ distance) for i in range(size)])


def shards(
    wide,
    narrow,
    residual_in,
    query_nope,
    query_rope,
    absorb_key,
    absorb_value,
    latent_cache,
    cache_lengths,
    slot_rows,
    out_proj,
    norm_gain,
    gate_weight,
    up_weight,
    down_weight,
):
    slots, heads, head_size = query_nope.shape
    rope = query_rope.shape[2]
    features = out_proj.shape[1]
    rows = slot_rows.shape[0]
    per_block = out_proj.shape[0] // head_size
    blocks = heads // per_block
    group = lax.axis_index("wide").astype(jnp.int32)
    scale = 1.0 / math.sqrt(head_size + rope)

    packed = call(
        pack_kernel,
        pltpu.VMEM((wide, slots, heads, head_size + 128), BF16),
        [SMEM, HBM, HBM],
        "pack",
        [
            pltpu.VMEM(query_nope.shape, BF16),
            pltpu.VMEM(query_rope.shape, BF16),
            pltpu.SemaphoreType.DMA((2,)),
        ],
        flops=PACK,
    )(group[None], far(query_nope), far(query_rope))
    queries = lax.all_to_all(packed, "wide", 0, 0, tiled=True)
    cache = jnp.swapaxes(latent_cache, 1, 2)
    heads_out = call(
        functools.partial(attend_kernel, narrow, blocks, scale),
        pltpu.VMEM((wide * narrow, slots * per_block, head_size), BF16),
        [SMEM, SMEM, SMEM, VMEM, VMEM, VMEM, VMEM],
        "attend",
        flops=ATTEND,
    )(
        group[None],
        slot_rows,
        cache_lengths,
        queries,
        near(absorb_key),
        near(cache),
        near(absorb_value),
    )
    received = lax.all_to_all(heads_out, ("wide", "narrow"), 0, 0, tiled=True)
    summed = call(
        functools.partial(project_kernel, narrow, blocks),
        pltpu.VMEM((rows, features), BF16),
        [SMEM, SMEM, VMEM, VMEM, VMEM],
        "project",
        flops=PROJECT,
    )(slot_rows, group[None], received, residual_in, out_proj)
    distance = 1
    while distance < wide:
        other = swap(summed, "wide", distance, wide)
        distance *= 2
        if distance < wide:
            summed = (summed.astype(F32) + other.astype(F32)).astype(BF16)
    columns = gate_weight.shape[1]
    padded = -(-columns // 128) * 128
    middle, terms = call(
        expand_kernel,
        (
            pltpu.VMEM((slots, features), F32),
            pltpu.VMEM((rows, 2 * padded + 256), BF16),
        ),
        [SMEM] + [VMEM] * 5,
        "expand",
        flops=EXPAND,
    )(group[None], summed, other, norm_gain[None, :], gate_weight, up_weight)
    distance = 1
    while distance < narrow:
        other = swap(terms, "narrow", distance, narrow)
        distance *= 2
        if distance < narrow:
            terms = call(merge_kernel, terms_like(terms), [VMEM] * 2, "merge", flops=MERGE)(terms, other)
    down = call(
        contract_kernel,
        pltpu.VMEM((wide, slots, features), F32),
        [VMEM] * 3,
        "contract",
        flops=CONTRACT,
    )(terms, other, down_weight)
    total = jnp.sum(lax.all_to_all(down, "wide", 0, 0, tiled=True), axis=0)
    return (middle + total).astype(BF16)


def terms_like(array):
    return pltpu.VMEM(array.shape, array.dtype)


def solution(mesh):
    in_specs = (
        P("wide", "narrow"),
        P("wide", "narrow", None),
        P("wide", "narrow", None),
        P("narrow", None, None),
        P("narrow", None, None),
        P("wide", None, None),
        P("wide"),
        P(),
        P("wide", "narrow"),
        P("narrow"),
        P("narrow", "wide"),
        P("narrow", "wide"),
        P("wide", "narrow"),
    )
    out_specs = P("wide", "narrow")
    body = functools.partial(shards, mesh.shape["wide"], mesh.shape["narrow"])
    return jax.shard_map(body, mesh=mesh, in_specs=in_specs, out_specs=out_specs, check_vma=False)
```

```python
import functools
import math

import jax
import jax.numpy as jnp
from jax import lax
from jax.experimental import pallas as pl
from jax.experimental.pallas import tpu as pltpu
from jax.sharding import PartitionSpec as P

D = 7168
BF16 = jnp.bfloat16
F32 = jnp.float32
VMEM = pl.BlockSpec(memory_space=pltpu.VMEM)
SMEM = pl.BlockSpec(memory_space=pltpu.SMEM)
HBM = pl.BlockSpec(memory_space=pltpu.HBM)
NT = (((1,), (1,)), ((), ()))


PACK = 10 * 10**9
ATTEND = 15 * 10**9
PROJECT = 12 * 10**9
EXPAND = 4 * 10**9
MERGE = 4 * 10**9
CONTRACT = 4 * 10**9


def near(array):
    return pltpu.with_memory_space_constraint(array, pltpu.VMEM)


def far(array):
    return pltpu.with_memory_space_constraint(array, pltpu.HBM)


def call(kernel, out_shape, in_specs, name, scratch=(), flops=0):
    return pl.pallas_call(
        kernel,
        out_shape=out_shape,
        scratch_shapes=scratch,
        cost_estimate=pl.CostEstimate(flops=flops, transcendentals=0, bytes_accessed=0),
        in_specs=in_specs,
        out_specs=jax.tree.map(lambda _: VMEM, out_shape),
        compiler_params=pltpu.CompilerParams(vmem_limit_bytes=16 * 1024 * 1024),
        name=name,
    )


def pack_kernel(group_ref, nope_hbm, rope_hbm, out_ref, nope_ref, rope_ref, sems):
    copies = [
        pltpu.make_async_copy(nope_hbm, nope_ref, sems.at[0]),
        pltpu.make_async_copy(rope_hbm, rope_ref, sems.at[1]),
    ]
    for copy in copies:
        copy.start()
    head_size, width = nope_ref.shape[2], rope_ref.shape[2]
    empty = jnp.zeros(rope_ref.shape[:2] + (out_ref.shape[3] - head_size - width,), BF16)
    for copy in copies:
        copy.wait()
    row = jnp.concatenate([nope_ref[...], rope_ref[...], empty], axis=2)
    for target in range(out_ref.shape[0]):
        out_ref[target] = row


def attend_kernel(
    narrow,
    blocks,
    scale,
    group_ref,
    rows_ref,
    lengths_ref,
    query_ref,
    key_ref,
    cache_ref,
    value_ref,
    out_ref,
):
    slots, latent = cache_ref.shape[0], value_ref.shape[1]
    heads, head_size = key_ref.shape[0], key_ref.shape[1]
    rope = cache_ref.shape[1] - latent
    span = cache_ref.shape[2]
    group = group_ref[0]
    queries = []
    for slot in range(slots):
        row = rows_ref[group * slots + slot]
        queries.append(query_ref[row // slots, row % slots])
    query = jnp.concatenate(queries, axis=0)
    own_head = lax.broadcasted_iota(jnp.int32, (slots * heads, 1), 0) % heads
    nope = query[:, :head_size]
    zero = jnp.zeros((), BF16)
    spread = jnp.concatenate(
        [jnp.where(own_head == head, nope, zero) for head in range(heads)], axis=1
    )
    query_latent = jnp.dot(
        spread, key_ref[...].reshape(heads * head_size, latent), preferred_element_type=F32
    ).astype(BF16)
    contexts = []
    for slot in range(slots):
        part = slice(slot * heads, (slot + 1) * heads)
        scores = jnp.dot(
            query_latent[part], cache_ref[slot, :latent, :], preferred_element_type=F32
        ) + jnp.dot(
            query[part, head_size : head_size + rope],
            cache_ref[slot, latent:, :],
            preferred_element_type=F32,
        )
        live = lax.broadcasted_iota(jnp.int32, (1, span), 1) < lengths_ref[slot]
        scores = jnp.where(live, scores * scale, -jnp.inf)
        weights = jnp.exp(scores - jnp.max(scores, axis=1, keepdims=True))
        probs = (weights / jnp.sum(weights, axis=1, keepdims=True)).astype(BF16)
        contexts.append(
            lax.dot_general(
                probs, cache_ref[slot, :latent, :], NT, preferred_element_type=F32
            ).astype(BF16)
        )
    context = jnp.concatenate(contexts, axis=0)
    spread = jnp.concatenate(
        [jnp.where(own_head == head, context, zero) for head in range(heads)], axis=1
    )
    heads_out = jnp.dot(
        spread, value_ref[...].reshape(heads * latent, head_size), preferred_element_type=F32
    ).astype(BF16)
    per_block = heads // blocks
    pieces = []
    for block in range(blocks):
        low = block * per_block
        pieces.append(
            jnp.concatenate(
                [
                    heads_out[slot * heads + low : slot * heads + low + per_block]
                    for slot in range(slots)
                ],
                axis=0,
            )
        )
    for target in range(out_ref.shape[0]):
        out_ref[target] = pieces[(target // narrow) % blocks]


def project_kernel(narrow, blocks, rows_ref, group_ref, heads_ref, residual_ref, weight_ref, out_ref):
    wide = heads_ref.shape[0] // narrow
    slots = residual_ref.shape[0]
    rows = wide * slots
    per_block = heads_ref.shape[1] // slots
    head_size = heads_ref.shape[2]
    group = group_ref[0]
    holder = group // blocks
    received = jnp.concatenate(
        [heads_ref[source * narrow + holder] for source in range(wide)], axis=0
    )
    count = rows * per_block
    column = lax.broadcasted_iota(jnp.int32, (1, count), 1)
    column_row = jnp.zeros((1, count), jnp.int32)
    for slot in range(rows):
        column_row = jnp.where(column // per_block == slot, rows_ref[slot], column_row)
    wanted = column_row + rows * (column % per_block)
    position = lax.broadcasted_iota(jnp.int32, (count, count), 0)
    select = jnp.where(position == wanted, 1.0, 0.0).astype(BF16)
    ordered = jnp.dot(select, received, preferred_element_type=F32).astype(BF16)
    flat = jnp.concatenate(
        [ordered[head * rows : (head + 1) * rows] for head in range(per_block)], axis=1
    )
    total = jnp.dot(flat, weight_ref[...], preferred_element_type=F32)
    row = lax.broadcasted_iota(jnp.int32, (rows, 1), 0)
    for slot in range(slots):
        own = residual_ref[slot : slot + 1, :].astype(F32)
        total = total + jnp.where(row == group * slots + slot, own, 0.0)
    out_ref[...] = total.astype(BF16)


def split_sum(value):
    high = value.astype(BF16)
    low = (value - high.astype(F32)).astype(BF16)
    return high, low


def put_sums(out_ref, start, value):
    high, low = split_sum(value)
    shape = (value.shape[0], 128)
    out_ref[:, start : start + 128] = jnp.broadcast_to(high, shape)
    out_ref[:, start + 128 : start + 256] = jnp.broadcast_to(low, shape)


def get_sums(ref, start):
    return ref[:, start : start + 1].astype(F32) + ref[:, start + 128 : start + 129].astype(F32)


def gate_kernel(
    group_ref, first_ref, second_ref, gain_ref, weight_ref, middle_ref, scaled_ref, out_ref
):
    middle = first_ref[...].astype(F32) + second_ref[...].astype(F32)
    slots = middle_ref.shape[0]
    row = lax.broadcasted_iota(jnp.int32, (middle.shape[0], 1), 0)
    for slot in range(slots):
        own = jnp.where(row == group_ref[0] * slots + slot, middle, 0.0)
        middle_ref[slot : slot + 1] = jnp.sum(own, axis=0, keepdims=True)
    scaled = (middle * gain_ref[...].astype(F32)).astype(BF16)
    scaled_ref[...] = scaled
    columns = weight_ref.shape[1]
    out_ref[:, :columns] = jnp.dot(scaled, weight_ref[...], preferred_element_type=F32).astype(BF16)
    put_sums(out_ref, out_ref.shape[1] - 256, jnp.sum(middle * middle, axis=1, keepdims=True))


def up_kernel(scaled_ref, weight_ref, out_ref):
    out_ref[...] = jnp.dot(scaled_ref[...], weight_ref[...], preferred_element_type=F32).astype(
        BF16
    )


def merge_kernel(first_ref, second_ref, out_ref):
    out_ref[...] = (first_ref[...].astype(F32) + second_ref[...].astype(F32)).astype(BF16)


def merge_sums_kernel(first_ref, second_ref, out_ref):
    end = out_ref.shape[1] - 256
    out_ref[:, :end] = (
        first_ref[:, :end].astype(F32) + second_ref[:, :end].astype(F32)
    ).astype(BF16)
    put_sums(out_ref, end, get_sums(first_ref, end) + get_sums(second_ref, end))


def contract_kernel(
    first_gate_ref, second_gate_ref, first_up_ref, second_up_ref, weight_ref, out_ref
):
    end = first_gate_ref.shape[1] - 256
    columns = weight_ref.shape[0]
    square = get_sums(first_gate_ref, end) + get_sums(second_gate_ref, end)
    factor = lax.rsqrt(square / D + 1e-06)
    gate = first_gate_ref[:, :columns].astype(F32) + second_gate_ref[:, :columns].astype(F32)
    gate = gate * factor
    up = (first_up_ref[...].astype(F32) + second_up_ref[...].astype(F32)) * factor
    hidden = (gate / (1.0 + jnp.exp(-gate)) * up).astype(BF16)
    total = jnp.dot(hidden, weight_ref[...], preferred_element_type=F32)
    slots = out_ref.shape[1]
    for owner in range(out_ref.shape[0]):
        out_ref[owner] = total[owner * slots : (owner + 1) * slots]


def swap(array, axis, distance, size):
    return lax.ppermute(array, axis, [(i, i ^ distance) for i in range(size)])


def shards(
    wide,
    narrow,
    residual_in,
    query_nope,
    query_rope,
    absorb_key,
    absorb_value,
    latent_cache,
    cache_lengths,
    slot_rows,
    out_proj,
    norm_gain,
    gate_weight,
    up_weight,
    down_weight,
):
    slots, heads, head_size = query_nope.shape
    rope = query_rope.shape[2]
    features = out_proj.shape[1]
    rows = slot_rows.shape[0]
    per_block = out_proj.shape[0] // head_size
    blocks = heads // per_block
    group = lax.axis_index("wide").astype(jnp.int32)
    scale = 1.0 / math.sqrt(head_size + rope)

    packed = call(
        pack_kernel,
        pltpu.VMEM((wide, slots, heads, head_size + 128), BF16),
        [SMEM, HBM, HBM],
        "pack",
        [
            pltpu.VMEM(query_nope.shape, BF16),
            pltpu.VMEM(query_rope.shape, BF16),
            pltpu.SemaphoreType.DMA((2,)),
        ],
        flops=PACK,
    )(group[None], far(query_nope), far(query_rope))
    queries = lax.all_to_all(packed, "wide", 0, 0, tiled=True)
    cache = jnp.swapaxes(latent_cache, 1, 2)
    heads_out = call(
        functools.partial(attend_kernel, narrow, blocks, scale),
        pltpu.VMEM((wide * narrow, slots * per_block, head_size), BF16),
        [SMEM, SMEM, SMEM, VMEM, VMEM, VMEM, VMEM],
        "attend",
        flops=ATTEND,
    )(
        group[None],
        slot_rows,
        cache_lengths,
        queries,
        near(absorb_key),
        near(cache),
        near(absorb_value),
    )
    received = lax.all_to_all(heads_out, ("wide", "narrow"), 0, 0, tiled=True)
    summed = call(
        functools.partial(project_kernel, narrow, blocks),
        pltpu.VMEM((rows, features), BF16),
        [SMEM, SMEM, VMEM, VMEM, VMEM],
        "project",
        flops=PROJECT,
    )(slot_rows, group[None], received, residual_in, out_proj)
    distance = 1
    while distance < wide:
        other = swap(summed, "wide", distance, wide)
        distance *= 2
        if distance < wide:
            summed = (summed.astype(F32) + other.astype(F32)).astype(BF16)
    columns = gate_weight.shape[1]
    padded = -(-columns // 128) * 128
    gate_shape = pltpu.VMEM((rows, padded + 256), BF16)
    up_shape = pltpu.VMEM((rows, columns), BF16)
    middle, scaled, gate = call(
        gate_kernel,
        (pltpu.VMEM((slots, features), F32), pltpu.VMEM((rows, features), BF16), gate_shape),
        [SMEM] + [VMEM] * 4,
        "gate",
        flops=EXPAND // 2,
    )(group[None], summed, other, norm_gain[None, :], gate_weight)
    up = call(up_kernel, up_shape, [VMEM] * 2, "up", flops=EXPAND // 2)(scaled, up_weight)
    distance = 1
    while distance < narrow:
        other_gate = swap(gate, "narrow", distance, narrow)
        other_up = swap(up, "narrow", distance, narrow)
        distance *= 2
        if distance < narrow:
            gate = call(
                merge_sums_kernel, gate_shape, [VMEM] * 2, "merge_gate", flops=MERGE // 4
            )(gate, other_gate)
            up = call(merge_kernel, up_shape, [VMEM] * 2, "merge_up", flops=MERGE // 4)(
                up, other_up
            )
    down = call(
        contract_kernel,
        pltpu.VMEM((wide, slots, features), F32),
        [VMEM] * 5,
        "contract",
        flops=CONTRACT,
    )(gate, other_gate, up, other_up, down_weight)
    total = jnp.sum(lax.all_to_all(down, "wide", 0, 0, tiled=True), axis=0)
    return (middle + total).astype(BF16)


def solution(mesh):
    in_specs = (
        P("wide", "narrow"),
        P("wide", "narrow", None),
        P("wide", "narrow", None),
        P("narrow", None, None),
        P("narrow", None, None),
        P("wide", None, None),
        P("wide"),
        P(),
        P("wide", "narrow"),
        P("narrow"),
        P("narrow", "wide"),
        P("narrow", "wide"),
        P("wide", "narrow"),
    )
    out_specs = P("wide", "narrow")
    body = functools.partial(shards, mesh.shape["wide"], mesh.shape["narrow"])
    return jax.shard_map(body, mesh=mesh, in_specs=in_specs, out_specs=out_specs, check_vma=False)
```

```python
import functools
import math

import jax
import jax.numpy as jnp
from jax import lax
from jax.experimental import pallas as pl
from jax.experimental.pallas import tpu as pltpu
from jax.sharding import PartitionSpec as P

D = 7168
BF16 = jnp.bfloat16
F32 = jnp.float32
VMEM = pl.BlockSpec(memory_space=pltpu.VMEM)
SMEM = pl.BlockSpec(memory_space=pltpu.SMEM)
HBM = pl.BlockSpec(memory_space=pltpu.HBM)
NT = (((1,), (1,)), ((), ()))


PACK = 10 * 10**9
ATTEND = 15 * 10**9
PROJECT = 12 * 10**9
EXPAND = 4 * 10**9
MERGE = 4 * 10**9
CONTRACT = 4 * 10**9


def near(array):
    return pltpu.with_memory_space_constraint(array, pltpu.VMEM)


def far(array):
    return pltpu.with_memory_space_constraint(array, pltpu.HBM)


def call(kernel, out_shape, in_specs, name, scratch=(), flops=0):
    return pl.pallas_call(
        kernel,
        out_shape=out_shape,
        scratch_shapes=scratch,
        cost_estimate=pl.CostEstimate(flops=flops, transcendentals=0, bytes_accessed=0),
        in_specs=in_specs,
        out_specs=jax.tree.map(lambda _: VMEM, out_shape),
        compiler_params=pltpu.CompilerParams(vmem_limit_bytes=16 * 1024 * 1024),
        name=name,
    )


def pack_kernel(group_ref, nope_hbm, rope_hbm, out_ref, nope_ref, rope_ref, sems):
    copies = [
        pltpu.make_async_copy(nope_hbm, nope_ref, sems.at[0]),
        pltpu.make_async_copy(rope_hbm, rope_ref, sems.at[1]),
    ]
    for copy in copies:
        copy.start()
    heads = nope_ref.shape[1]
    for copy in copies:
        copy.wait()
    pairs = jnp.concatenate([rope_ref[:, : heads // 2], rope_ref[:, heads // 2 :]], axis=2)
    row = jnp.concatenate([nope_ref[...], pairs], axis=1)
    for target in range(out_ref.shape[0]):
        out_ref[target] = row


def attend_kernel(
    narrow,
    blocks,
    scale,
    group_ref,
    rows_ref,
    lengths_ref,
    query_ref,
    key_ref,
    cache_ref,
    value_ref,
    out_ref,
):
    slots, latent = cache_ref.shape[0], value_ref.shape[1]
    heads, head_size = key_ref.shape[0], key_ref.shape[1]
    rope = cache_ref.shape[1] - latent
    span = cache_ref.shape[2]
    group = group_ref[0]
    queries = []
    for slot in range(slots):
        row = rows_ref[group * slots + slot]
        queries.append(query_ref[row // slots, row % slots])
    nope = jnp.concatenate([query[:heads] for query in queries], axis=0)
    ropes = [
        jnp.concatenate([query[heads:, :rope], query[heads:, rope:]], axis=0) for query in queries
    ]
    own_head = lax.broadcasted_iota(jnp.int32, (slots * heads, 1), 0) % heads
    total = jnp.zeros((slots * heads, latent), F32)
    for head in range(heads):
        term = jnp.dot(nope, key_ref[head], preferred_element_type=F32)
        total = jnp.where(own_head == head, term, total)
    query_latent = total.astype(BF16)
    parts = [slice(slot * heads, (slot + 1) * heads) for slot in range(slots)]
    scores = [
        jnp.dot(query_latent[part], cache_ref[slot, :latent, :], preferred_element_type=F32)
        + jnp.dot(
            ropes[slot],
            cache_ref[slot, latent:, :],
            preferred_element_type=F32,
        )
        for slot, part in enumerate(parts)
    ]
    probs = []
    for slot in range(slots):
        live = lax.broadcasted_iota(jnp.int32, (1, span), 1) < lengths_ref[slot]
        masked = jnp.where(live, scores[slot] * scale, -jnp.inf)
        weights = jnp.exp(masked - jnp.max(masked, axis=1, keepdims=True))
        probs.append((weights / jnp.sum(weights, axis=1, keepdims=True)).astype(BF16))
    context = jnp.concatenate(
        [
            lax.dot_general(
                probs[slot], cache_ref[slot, :latent, :], NT, preferred_element_type=F32
            ).astype(BF16)
            for slot in range(slots)
        ],
        axis=0,
    )
    total = jnp.zeros((slots * heads, head_size), F32)
    for head in range(heads):
        term = jnp.dot(context, value_ref[head], preferred_element_type=F32)
        total = jnp.where(own_head == head, term, total)
    heads_out = total.astype(BF16)
    per_block = heads // blocks
    pieces = []
    for block in range(blocks):
        low = block * per_block
        pieces.append(
            jnp.concatenate(
                [
                    heads_out[slot * heads + low : slot * heads + low + per_block]
                    for slot in range(slots)
                ],
                axis=0,
            )
        )
    for target in range(out_ref.shape[0]):
        out_ref[target] = pieces[(target // narrow) % blocks]


def project_kernel(narrow, blocks, rows_ref, group_ref, heads_ref, residual_ref, weight_ref, out_ref):
    wide = heads_ref.shape[0] // narrow
    slots = residual_ref.shape[0]
    rows = wide * slots
    per_block = heads_ref.shape[1] // slots
    head_size = heads_ref.shape[2]
    group = group_ref[0]
    holder = group // blocks
    received = jnp.concatenate(
        [heads_ref[source * narrow + holder] for source in range(wide)], axis=0
    )
    count = rows * per_block
    column = lax.broadcasted_iota(jnp.int32, (1, count), 1)
    column_row = jnp.zeros((1, count), jnp.int32)
    for slot in range(rows):
        column_row = jnp.where(column // per_block == slot, rows_ref[slot], column_row)
    wanted = column_row + rows * (column % per_block)
    position = lax.broadcasted_iota(jnp.int32, (count, count), 0)
    select = jnp.where(position == wanted, 1.0, 0.0).astype(BF16)
    ordered = jnp.dot(select, received, preferred_element_type=F32).astype(BF16)
    flat = jnp.concatenate(
        [ordered[head * rows : (head + 1) * rows] for head in range(per_block)], axis=1
    )
    total = jnp.dot(flat, weight_ref[...], preferred_element_type=F32)
    row = lax.broadcasted_iota(jnp.int32, (rows, 1), 0)
    for slot in range(slots):
        own = residual_ref[slot : slot + 1, :].astype(F32)
        total = total + jnp.where(row == group * slots + slot, own, 0.0)
    out_ref[...] = total.astype(BF16)


def split_sum(value):
    high = value.astype(BF16)
    low = (value - high.astype(F32)).astype(BF16)
    return high, low


def put_sums(out_ref, start, value):
    high, low = split_sum(value)
    shape = (value.shape[0], 128)
    out_ref[:, start : start + 128] = jnp.broadcast_to(high, shape)
    out_ref[:, start + 128 : start + 256] = jnp.broadcast_to(low, shape)


def get_sums(ref, start):
    return ref[:, start : start + 1].astype(F32) + ref[:, start + 128 : start + 129].astype(F32)


def gate_kernel(
    group_ref, first_ref, second_ref, gain_ref, weight_ref, middle_ref, scaled_ref, out_ref
):
    middle = first_ref[...].astype(F32) + second_ref[...].astype(F32)
    slots = middle_ref.shape[0]
    row = lax.broadcasted_iota(jnp.int32, (middle.shape[0], 1), 0)
    for slot in range(slots):
        own = jnp.where(row == group_ref[0] * slots + slot, middle, 0.0)
        middle_ref[slot : slot + 1] = jnp.sum(own, axis=0, keepdims=True)
    scaled = (middle * gain_ref[...].astype(F32)).astype(BF16)
    scaled_ref[...] = scaled
    columns = weight_ref.shape[1]
    out_ref[:, :columns] = jnp.dot(scaled, weight_ref[...], preferred_element_type=F32).astype(BF16)
    put_sums(out_ref, out_ref.shape[1] - 256, jnp.sum(middle * middle, axis=1, keepdims=True))


def up_kernel(scaled_ref, weight_ref, out_ref):
    out_ref[...] = jnp.dot(scaled_ref[...], weight_ref[...], preferred_element_type=F32).astype(
        BF16
    )


def merge_kernel(first_ref, second_ref, out_ref):
    out_ref[...] = (first_ref[...].astype(F32) + second_ref[...].astype(F32)).astype(BF16)


def merge_sums_kernel(first_ref, second_ref, out_ref):
    end = out_ref.shape[1] - 256
    out_ref[:, :end] = (
        first_ref[:, :end].astype(F32) + second_ref[:, :end].astype(F32)
    ).astype(BF16)
    put_sums(out_ref, end, get_sums(first_ref, end) + get_sums(second_ref, end))


def contract_kernel(
    first_gate_ref, second_gate_ref, first_up_ref, second_up_ref, weight_ref, out_ref
):
    end = first_gate_ref.shape[1] - 256
    columns = weight_ref.shape[0]
    square = get_sums(first_gate_ref, end) + get_sums(second_gate_ref, end)
    factor = lax.rsqrt(square / D + 1e-06)
    gate = first_gate_ref[:, :columns].astype(F32) + second_gate_ref[:, :columns].astype(F32)
    gate = gate * factor
    up = (first_up_ref[...].astype(F32) + second_up_ref[...].astype(F32)) * factor
    hidden = (gate / (1.0 + jnp.exp(-gate)) * up).astype(BF16)
    total = jnp.dot(hidden, weight_ref[...], preferred_element_type=F32)
    slots = out_ref.shape[1]
    for owner in range(out_ref.shape[0]):
        out_ref[owner] = total[owner * slots : (owner + 1) * slots]


def swap(array, axis, distance, size):
    return lax.ppermute(array, axis, [(i, i ^ distance) for i in range(size)])


def shards(
    wide,
    narrow,
    residual_in,
    query_nope,
    query_rope,
    absorb_key,
    absorb_value,
    latent_cache,
    cache_lengths,
    slot_rows,
    out_proj,
    norm_gain,
    gate_weight,
    up_weight,
    down_weight,
):
    slots, heads, head_size = query_nope.shape
    rope = query_rope.shape[2]
    features = out_proj.shape[1]
    rows = slot_rows.shape[0]
    per_block = out_proj.shape[0] // head_size
    blocks = heads // per_block
    group = lax.axis_index("wide").astype(jnp.int32)
    scale = 1.0 / math.sqrt(head_size + rope)

    packed = call(
        pack_kernel,
        pltpu.VMEM((wide, slots, heads + heads // 2, head_size), BF16),
        [SMEM, HBM, HBM],
        "pack",
        [
            pltpu.VMEM(query_nope.shape, BF16),
            pltpu.VMEM(query_rope.shape, BF16),
            pltpu.SemaphoreType.DMA((2,)),
        ],
        flops=PACK,
    )(group[None], far(query_nope), far(query_rope))
    queries = lax.all_to_all(packed, "wide", 0, 0, tiled=True)
    cache = jnp.swapaxes(latent_cache, 1, 2)
    heads_out = call(
        functools.partial(attend_kernel, narrow, blocks, scale),
        pltpu.VMEM((wide * narrow, slots * per_block, head_size), BF16),
        [SMEM, SMEM, SMEM, VMEM, VMEM, VMEM, VMEM],
        "attend",
        flops=ATTEND,
    )(
        group[None],
        slot_rows,
        cache_lengths,
        queries,
        near(absorb_key),
        near(cache),
        near(absorb_value),
    )
    received = lax.all_to_all(heads_out, ("wide", "narrow"), 0, 0, tiled=True)
    summed = call(
        functools.partial(project_kernel, narrow, blocks),
        pltpu.VMEM((rows, features), BF16),
        [SMEM, SMEM, VMEM, VMEM, VMEM],
        "project",
        flops=PROJECT,
    )(slot_rows, group[None], received, residual_in, out_proj)
    distance = 1
    while distance < wide:
        other = swap(summed, "wide", distance, wide)
        distance *= 2
        if distance < wide:
            summed = (summed.astype(F32) + other.astype(F32)).astype(BF16)
    columns = gate_weight.shape[1]
    padded = -(-columns // 128) * 128
    gate_shape = pltpu.VMEM((rows, padded + 256), BF16)
    up_shape = pltpu.VMEM((rows, columns), BF16)
    middle, scaled, gate = call(
        gate_kernel,
        (pltpu.VMEM((slots, features), F32), pltpu.VMEM((rows, features), BF16), gate_shape),
        [SMEM] + [VMEM] * 4,
        "gate",
        flops=EXPAND // 2,
    )(group[None], summed, other, norm_gain[None, :], gate_weight)
    up = call(up_kernel, up_shape, [VMEM] * 2, "up", flops=EXPAND // 2)(scaled, up_weight)
    distance = 1
    while distance < narrow:
        other_gate = swap(gate, "narrow", distance, narrow)
        other_up = swap(up, "narrow", distance, narrow)
        distance *= 2
        if distance < narrow:
            gate = call(
                merge_sums_kernel, gate_shape, [VMEM] * 2, "merge_gate", flops=MERGE // 4
            )(gate, other_gate)
            up = call(merge_kernel, up_shape, [VMEM] * 2, "merge_up", flops=MERGE // 4)(
                up, other_up
            )
    down = call(
        contract_kernel,
        pltpu.VMEM((wide, slots, features), F32),
        [VMEM] * 5,
        "contract",
        flops=CONTRACT,
    )(gate, other_gate, up, other_up, down_weight)
    total = jnp.sum(lax.all_to_all(down, "wide", 0, 0, tiled=True), axis=0)
    return (middle + total).astype(BF16)


def solution(mesh):
    in_specs = (
        P("wide", "narrow"),
        P("wide", "narrow", None),
        P("wide", "narrow", None),
        P("narrow", None, None),
        P("narrow", None, None),
        P("wide", None, None),
        P("wide"),
        P(),
        P("wide", "narrow"),
        P("narrow"),
        P("narrow", "wide"),
        P("narrow", "wide"),
        P("wide", "narrow"),
    )
    out_specs = P("wide", "narrow")
    body = functools.partial(shards, mesh.shape["wide"], mesh.shape["narrow"])
    return jax.shard_map(body, mesh=mesh, in_specs=in_specs, out_specs=out_specs, check_vma=False)
```

```python
import functools
import math

import jax
import jax.numpy as jnp
from jax import lax
from jax.experimental import pallas as pl
from jax.experimental.pallas import tpu as pltpu
from jax.sharding import PartitionSpec as P

D = 7168
BF16 = jnp.bfloat16
F32 = jnp.float32
VMEM = pl.BlockSpec(memory_space=pltpu.VMEM)
SMEM = pl.BlockSpec(memory_space=pltpu.SMEM)
HBM = pl.BlockSpec(memory_space=pltpu.HBM)
NT = (((1,), (1,)), ((), ()))


PACK = 10 * 10**9
ATTEND = 15 * 10**9
PROJECT = 12 * 10**9
EXPAND = 4 * 10**9
MERGE = 4 * 10**9
CONTRACT = 4 * 10**9


def near(array):
    return pltpu.with_memory_space_constraint(array, pltpu.VMEM)


def far(array):
    return pltpu.with_memory_space_constraint(array, pltpu.HBM)


def call(kernel, out_shape, in_specs, name, scratch=(), flops=0):
    return pl.pallas_call(
        kernel,
        out_shape=out_shape,
        scratch_shapes=scratch,
        cost_estimate=pl.CostEstimate(flops=flops, transcendentals=0, bytes_accessed=0),
        in_specs=in_specs,
        out_specs=jax.tree.map(lambda _: VMEM, out_shape),
        compiler_params=pltpu.CompilerParams(vmem_limit_bytes=16 * 1024 * 1024),
        name=name,
    )


def pack_kernel(group_ref, nope_hbm, rope_hbm, out_ref, nope_ref, rope_ref, sems):
    copies = [
        pltpu.make_async_copy(nope_hbm, nope_ref, sems.at[0]),
        pltpu.make_async_copy(rope_hbm, rope_ref, sems.at[1]),
    ]
    for copy in copies:
        copy.start()
    heads = nope_ref.shape[1]
    for copy in copies:
        copy.wait()
    pairs = jnp.concatenate([rope_ref[:, : heads // 2], rope_ref[:, heads // 2 :]], axis=2)
    row = jnp.concatenate([nope_ref[...], pairs], axis=1)
    for target in range(out_ref.shape[0]):
        out_ref[target] = row


def attend_kernel(
    narrow,
    blocks,
    scale,
    group_ref,
    rows_ref,
    lengths_ref,
    query_ref,
    key_ref,
    cache_ref,
    value_ref,
    out_ref,
):
    slots, latent = cache_ref.shape[0], value_ref.shape[1]
    heads, head_size = key_ref.shape[0], key_ref.shape[1]
    rope = cache_ref.shape[1] - latent
    span = cache_ref.shape[2]
    group = group_ref[0]
    queries = []
    for slot in range(slots):
        row = rows_ref[group * slots + slot]
        queries.append(query_ref[row // slots, row % slots])
    nope = jnp.concatenate([query[:heads] for query in queries], axis=0)
    ropes = [
        jnp.concatenate([query[heads:, :rope], query[heads:, rope:]], axis=0) for query in queries
    ]
    own_head = lax.broadcasted_iota(jnp.int32, (slots * heads, 1), 0) % heads
    total = jnp.zeros((slots * heads, latent), F32)
    for head in range(heads):
        term = jnp.dot(nope, key_ref[head], preferred_element_type=F32)
        total = jnp.where(own_head == head, term, total)
    query_latent = total.astype(BF16)
    parts = [slice(slot * heads, (slot + 1) * heads) for slot in range(slots)]
    scores = [
        jnp.dot(query_latent[part], cache_ref[slot, :latent, :], preferred_element_type=F32)
        + jnp.dot(
            ropes[slot],
            cache_ref[slot, latent:, :],
            preferred_element_type=F32,
        )
        for slot, part in enumerate(parts)
    ]
    probs = []
    for slot in range(slots):
        live = lax.broadcasted_iota(jnp.int32, (1, span), 1) < lengths_ref[slot]
        masked = jnp.where(live, scores[slot] * scale, -jnp.inf)
        weights = jnp.exp(masked - jnp.max(masked, axis=1, keepdims=True))
        probs.append((weights / jnp.sum(weights, axis=1, keepdims=True)).astype(BF16))
    context = jnp.concatenate(
        [
            lax.dot_general(
                probs[slot], cache_ref[slot, :latent, :], NT, preferred_element_type=F32
            ).astype(BF16)
            for slot in range(slots)
        ],
        axis=0,
    )
    total = jnp.zeros((slots * heads, head_size), F32)
    for head in range(heads):
        term = jnp.dot(context, value_ref[head], preferred_element_type=F32)
        total = jnp.where(own_head == head, term, total)
    heads_out = total.astype(BF16)
    per_block = heads // blocks
    pieces = []
    for block in range(blocks):
        low = block * per_block
        pieces.append(
            jnp.concatenate(
                [
                    heads_out[slot * heads + low : slot * heads + low + per_block]
                    for slot in range(slots)
                ],
                axis=0,
            )
        )
    for target in range(out_ref.shape[0]):
        out_ref[target] = pieces[(target // narrow) % blocks]


def project_kernel(narrow, blocks, rows_ref, group_ref, heads_ref, residual_ref, weight_ref, out_ref):
    wide = heads_ref.shape[0] // narrow
    slots = residual_ref.shape[0]
    rows = wide * slots
    per_block = heads_ref.shape[1] // slots
    head_size = heads_ref.shape[2]
    group = group_ref[0]
    holder = group // blocks
    received = jnp.concatenate(
        [heads_ref[source * narrow + holder] for source in range(wide)], axis=0
    )
    count = rows * per_block
    column = lax.broadcasted_iota(jnp.int32, (1, count), 1)
    column_row = jnp.zeros((1, count), jnp.int32)
    for slot in range(rows):
        column_row = jnp.where(column // per_block == slot, rows_ref[slot], column_row)
    wanted = column_row + rows * (column % per_block)
    position = lax.broadcasted_iota(jnp.int32, (count, count), 0)
    select = jnp.where(position == wanted, 1.0, 0.0).astype(BF16)
    ordered = jnp.dot(select, received, preferred_element_type=F32).astype(BF16)
    flat = jnp.concatenate(
        [ordered[head * rows : (head + 1) * rows] for head in range(per_block)], axis=1
    )
    total = jnp.dot(flat, weight_ref[...], preferred_element_type=F32)
    row = lax.broadcasted_iota(jnp.int32, (rows, 1), 0)
    for slot in range(slots):
        own = residual_ref[slot : slot + 1, :].astype(F32)
        total = total + jnp.where(row == group * slots + slot, own, 0.0)
    out_ref[...] = total.astype(BF16)


def split_sum(value):
    high = value.astype(BF16)
    low = (value - high.astype(F32)).astype(BF16)
    return high, low


def put_sums(out_ref, start, value):
    high, low = split_sum(value)
    shape = (value.shape[0], 128)
    out_ref[:, start : start + 128] = jnp.broadcast_to(high, shape)
    out_ref[:, start + 128 : start + 256] = jnp.broadcast_to(low, shape)


def get_sums(ref, start):
    return ref[:, start : start + 1].astype(F32) + ref[:, start + 128 : start + 129].astype(F32)


def gate_kernel(group_ref, gain_ref, weight_ref, *refs):
    parts, (middle_ref, scaled_ref, out_ref) = refs[:-3], refs[-3:]
    middle = parts[0][...].astype(F32)
    for part in parts[1:]:
        middle = middle + part[...].astype(F32)
    slots = middle_ref.shape[0]
    row = lax.broadcasted_iota(jnp.int32, (middle.shape[0], 1), 0)
    for slot in range(slots):
        own = jnp.where(row == group_ref[0] * slots + slot, middle, 0.0)
        middle_ref[slot : slot + 1] = jnp.sum(own, axis=0, keepdims=True)
    scaled = (middle * gain_ref[...].astype(F32)).astype(BF16)
    scaled_ref[...] = scaled
    columns = weight_ref.shape[1]
    out_ref[:, :columns] = jnp.dot(scaled, weight_ref[...], preferred_element_type=F32).astype(BF16)
    put_sums(out_ref, out_ref.shape[1] - 256, jnp.sum(middle * middle, axis=1, keepdims=True))


def up_kernel(scaled_ref, weight_ref, out_ref):
    out_ref[...] = jnp.dot(scaled_ref[...], weight_ref[...], preferred_element_type=F32).astype(
        BF16
    )


def merge_kernel(first_ref, second_ref, out_ref):
    out_ref[...] = (first_ref[...].astype(F32) + second_ref[...].astype(F32)).astype(BF16)


def merge_sums_kernel(first_ref, second_ref, out_ref):
    end = out_ref.shape[1] - 256
    out_ref[:, :end] = (
        first_ref[:, :end].astype(F32) + second_ref[:, :end].astype(F32)
    ).astype(BF16)
    put_sums(out_ref, end, get_sums(first_ref, end) + get_sums(second_ref, end))


def contract_kernel(
    first_gate_ref, second_gate_ref, first_up_ref, second_up_ref, weight_ref, out_ref
):
    end = first_gate_ref.shape[1] - 256
    columns = weight_ref.shape[0]
    square = get_sums(first_gate_ref, end) + get_sums(second_gate_ref, end)
    factor = lax.rsqrt(square / D + 1e-06)
    gate = first_gate_ref[:, :columns].astype(F32) + second_gate_ref[:, :columns].astype(F32)
    gate = gate * factor
    up = (first_up_ref[...].astype(F32) + second_up_ref[...].astype(F32)) * factor
    hidden = (gate / (1.0 + jnp.exp(-gate)) * up).astype(BF16)
    total = jnp.dot(hidden, weight_ref[...], preferred_element_type=F32)
    slots = out_ref.shape[1]
    for owner in range(out_ref.shape[0]):
        out_ref[owner] = total[owner * slots : (owner + 1) * slots]


def exchange_groups(size):
    bits = size.bit_length() - 1
    groups = [[1]] if bits else []
    for bit in range(1, bits, 2):
        groups.append([part << bit for part in range(1, 4 if bit + 1 < bits else 2)])
    return groups


def swap(array, axis, distance, size):
    return lax.ppermute(array, axis, [(i, i ^ distance) for i in range(size)])


def shards(
    wide,
    narrow,
    residual_in,
    query_nope,
    query_rope,
    absorb_key,
    absorb_value,
    latent_cache,
    cache_lengths,
    slot_rows,
    out_proj,
    norm_gain,
    gate_weight,
    up_weight,
    down_weight,
):
    slots, heads, head_size = query_nope.shape
    rope = query_rope.shape[2]
    features = out_proj.shape[1]
    rows = slot_rows.shape[0]
    per_block = out_proj.shape[0] // head_size
    blocks = heads // per_block
    group = lax.axis_index("wide").astype(jnp.int32)
    scale = 1.0 / math.sqrt(head_size + rope)

    packed = call(
        pack_kernel,
        pltpu.VMEM((wide, slots, heads + heads // 2, head_size), BF16),
        [SMEM, HBM, HBM],
        "pack",
        [
            pltpu.VMEM(query_nope.shape, BF16),
            pltpu.VMEM(query_rope.shape, BF16),
            pltpu.SemaphoreType.DMA((2,)),
        ],
        flops=PACK,
    )(group[None], far(query_nope), far(query_rope))
    queries = lax.all_to_all(packed, "wide", 0, 0, tiled=True)
    cache = jnp.swapaxes(latent_cache, 1, 2)
    heads_out = call(
        functools.partial(attend_kernel, narrow, blocks, scale),
        pltpu.VMEM((wide * narrow, slots * per_block, head_size), BF16),
        [SMEM, SMEM, SMEM, VMEM, VMEM, VMEM, VMEM],
        "attend",
        flops=ATTEND,
    )(
        group[None],
        slot_rows,
        cache_lengths,
        queries,
        near(absorb_key),
        near(cache),
        near(absorb_value),
    )
    received = lax.all_to_all(heads_out, ("wide", "narrow"), 0, 0, tiled=True)
    summed = call(
        functools.partial(project_kernel, narrow, blocks),
        pltpu.VMEM((rows, features), BF16),
        [SMEM, SMEM, VMEM, VMEM, VMEM],
        "project",
        flops=PROJECT,
    )(slot_rows, group[None], received, residual_in, out_proj)
    groups = exchange_groups(wide)
    for index, group_bits in enumerate(groups):
        others = [swap(summed, "wide", distance, wide) for distance in group_bits]
        if index + 1 < len(groups):
            total = summed.astype(F32)
            for other in others:
                total = total + other.astype(F32)
            summed = total.astype(BF16)
    columns = gate_weight.shape[1]
    padded = -(-columns // 128) * 128
    gate_shape = pltpu.VMEM((rows, padded + 256), BF16)
    up_shape = pltpu.VMEM((rows, columns), BF16)
    middle, scaled, gate = call(
        gate_kernel,
        (pltpu.VMEM((slots, features), F32), pltpu.VMEM((rows, features), BF16), gate_shape),
        [SMEM] + [VMEM] * (3 + len(others)),
        "gate",
        flops=EXPAND // 2,
    )(group[None], norm_gain[None, :], gate_weight, summed, *others)
    up = call(up_kernel, up_shape, [VMEM] * 2, "up", flops=EXPAND // 2)(scaled, up_weight)
    distance = 1
    while distance < narrow:
        other_gate = swap(gate, "narrow", distance, narrow)
        other_up = swap(up, "narrow", distance, narrow)
        distance *= 2
        if distance < narrow:
            gate = call(
                merge_sums_kernel, gate_shape, [VMEM] * 2, "merge_gate", flops=MERGE // 4
            )(gate, other_gate)
            up = call(merge_kernel, up_shape, [VMEM] * 2, "merge_up", flops=MERGE // 4)(
                up, other_up
            )
    down = call(
        contract_kernel,
        pltpu.VMEM((wide, slots, features), F32),
        [VMEM] * 5,
        "contract",
        flops=CONTRACT,
    )(gate, other_gate, up, other_up, down_weight)
    total = jnp.sum(lax.all_to_all(down, "wide", 0, 0, tiled=True), axis=0)
    return (middle + total).astype(BF16)


def solution(mesh):
    in_specs = (
        P("wide", "narrow"),
        P("wide", "narrow", None),
        P("wide", "narrow", None),
        P("narrow", None, None),
        P("narrow", None, None),
        P("wide", None, None),
        P("wide"),
        P(),
        P("wide", "narrow"),
        P("narrow"),
        P("narrow", "wide"),
        P("narrow", "wide"),
        P("wide", "narrow"),
    )
    out_specs = P("wide", "narrow")
    body = functools.partial(shards, mesh.shape["wide"], mesh.shape["narrow"])
    return jax.shard_map(body, mesh=mesh, in_specs=in_specs, out_specs=out_specs, check_vma=False)
```

```python
import functools
import math

import jax
import jax.numpy as jnp
from jax import lax
from jax.experimental import pallas as pl
from jax.experimental.pallas import tpu as pltpu
from jax.sharding import PartitionSpec as P

D = 7168
BF16 = jnp.bfloat16
F32 = jnp.float32
VMEM = pl.BlockSpec(memory_space=pltpu.VMEM)
SMEM = pl.BlockSpec(memory_space=pltpu.SMEM)
HBM = pl.BlockSpec(memory_space=pltpu.HBM)
NT = (((1,), (1,)), ((), ()))


PACK = 10 * 10**9
ATTEND = 15 * 10**9
PROJECT = 12 * 10**9
EXPAND = 4 * 10**9
MERGE = 4 * 10**9
CONTRACT = 4 * 10**9


def near(array):
    return pltpu.with_memory_space_constraint(array, pltpu.VMEM)


def far(array):
    return pltpu.with_memory_space_constraint(array, pltpu.HBM)


def call(kernel, out_shape, in_specs, name, scratch=(), flops=0):
    return pl.pallas_call(
        kernel,
        out_shape=out_shape,
        scratch_shapes=scratch,
        cost_estimate=pl.CostEstimate(flops=flops, transcendentals=0, bytes_accessed=0),
        in_specs=in_specs,
        out_specs=jax.tree.map(lambda _: VMEM, out_shape),
        compiler_params=pltpu.CompilerParams(vmem_limit_bytes=16 * 1024 * 1024),
        name=name,
    )


def pack_kernel(group_ref, nope_hbm, rope_hbm, out_ref, nope_ref, rope_ref, sems):
    copies = [
        pltpu.make_async_copy(nope_hbm, nope_ref, sems.at[0]),
        pltpu.make_async_copy(rope_hbm, rope_ref, sems.at[1]),
    ]
    for copy in copies:
        copy.start()
    heads = nope_ref.shape[1]
    for copy in copies:
        copy.wait()
    pairs = jnp.concatenate([rope_ref[:, : heads // 2], rope_ref[:, heads // 2 :]], axis=2)
    row = jnp.concatenate([nope_ref[...], pairs], axis=1)
    for target in range(out_ref.shape[0]):
        out_ref[target] = row


def attend_kernel(
    narrow,
    blocks,
    scale,
    group_ref,
    rows_ref,
    lengths_ref,
    query_ref,
    key_ref,
    cache_ref,
    value_ref,
    out_ref,
):
    slots, latent = cache_ref.shape[0], value_ref.shape[1]
    heads, head_size = key_ref.shape[0], key_ref.shape[1]
    rope = cache_ref.shape[1] - latent
    span = cache_ref.shape[2]
    group = group_ref[0]
    queries = []
    for slot in range(slots):
        row = rows_ref[group * slots + slot]
        queries.append(query_ref[row // slots, row % slots])
    nope = jnp.concatenate([query[:heads] for query in queries], axis=0)
    ropes = [
        jnp.concatenate([query[heads:, :rope], query[heads:, rope:]], axis=0) for query in queries
    ]
    own_head = lax.broadcasted_iota(jnp.int32, (slots * heads, 1), 0) % heads
    total = jnp.zeros((slots * heads, latent), F32)
    for head in range(heads):
        term = jnp.dot(nope, key_ref[head], preferred_element_type=F32)
        total = jnp.where(own_head == head, term, total)
    query_latent = total.astype(BF16)
    parts = [slice(slot * heads, (slot + 1) * heads) for slot in range(slots)]
    scores = [
        jnp.dot(query_latent[part], cache_ref[slot, :latent, :], preferred_element_type=F32)
        + jnp.dot(
            ropes[slot],
            cache_ref[slot, latent:, :],
            preferred_element_type=F32,
        )
        for slot, part in enumerate(parts)
    ]
    probs = []
    for slot in range(slots):
        live = lax.broadcasted_iota(jnp.int32, (1, span), 1) < lengths_ref[slot]
        masked = jnp.where(live, scores[slot] * scale, -jnp.inf)
        weights = jnp.exp(masked - jnp.max(masked, axis=1, keepdims=True))
        probs.append((weights / jnp.sum(weights, axis=1, keepdims=True)).astype(BF16))
    context = jnp.concatenate(
        [
            lax.dot_general(
                probs[slot], cache_ref[slot, :latent, :], NT, preferred_element_type=F32
            ).astype(BF16)
            for slot in range(slots)
        ],
        axis=0,
    )
    total = jnp.zeros((slots * heads, head_size), F32)
    for head in range(heads):
        term = jnp.dot(context, value_ref[head], preferred_element_type=F32)
        total = jnp.where(own_head == head, term, total)
    heads_out = total.astype(BF16)
    per_block = heads // blocks
    pieces = []
    for block in range(blocks):
        low = block * per_block
        pieces.append(
            jnp.concatenate(
                [
                    heads_out[slot * heads + low : slot * heads + low + per_block]
                    for slot in range(slots)
                ],
                axis=0,
            )
        )
    for target in range(out_ref.shape[0]):
        out_ref[target] = pieces[(target // narrow) % blocks]


def project_kernel(
    narrow, blocks, rows_ref, group_ref, heads_ref, residual_ref, weight_ref, own_ref, out_ref
):
    wide = heads_ref.shape[0] // narrow
    slots = residual_ref.shape[0]
    rows = wide * slots
    per_block = heads_ref.shape[1] // slots
    head_size = heads_ref.shape[2]
    group = group_ref[0]
    holder = group // blocks
    received = jnp.concatenate(
        [heads_ref[source * narrow + holder] for source in range(wide)], axis=0
    )
    count = rows * per_block
    column = lax.broadcasted_iota(jnp.int32, (1, count), 1)
    column_row = jnp.zeros((1, count), jnp.int32)
    for slot in range(rows):
        column_row = jnp.where(column // per_block == slot, rows_ref[slot], column_row)
    wanted = column_row + rows * (column % per_block)
    position = lax.broadcasted_iota(jnp.int32, (count, count), 0)
    select = jnp.where(position == wanted, 1.0, 0.0).astype(BF16)
    ordered = jnp.dot(select, received, preferred_element_type=F32).astype(BF16)
    flat = jnp.concatenate(
        [ordered[head * rows : (head + 1) * rows] for head in range(per_block)], axis=1
    )
    total = jnp.dot(flat, weight_ref[...], preferred_element_type=F32)
    row = lax.broadcasted_iota(jnp.int32, (rows, 1), 0)
    for slot in range(slots):
        own = residual_ref[slot : slot + 1, :].astype(F32)
        total = total + jnp.where(row == group * slots + slot, own, 0.0)
    own_ref[...] = total
    out_ref[...] = total.astype(BF16)


def split_sum(value):
    high = value.astype(BF16)
    low = (value - high.astype(F32)).astype(BF16)
    return high, low


def put_sums(out_ref, start, value):
    high, low = split_sum(value)
    shape = (value.shape[0], 128)
    out_ref[:, start : start + 128] = jnp.broadcast_to(high, shape)
    out_ref[:, start + 128 : start + 256] = jnp.broadcast_to(low, shape)


def get_sums(ref, start):
    return ref[:, start : start + 1].astype(F32) + ref[:, start + 128 : start + 129].astype(F32)


def gate_kernel(group_ref, gain_ref, weight_ref, *refs):
    parts, (middle_ref, scaled_ref, own_ref, out_ref) = refs[:-4], refs[-4:]
    middle = parts[0][...].astype(F32)
    for part in parts[1:]:
        middle = middle + part[...].astype(F32)
    slots = middle_ref.shape[0]
    row = lax.broadcasted_iota(jnp.int32, (middle.shape[0], 1), 0)
    for slot in range(slots):
        own = jnp.where(row == group_ref[0] * slots + slot, middle, 0.0)
        middle_ref[slot : slot + 1] = jnp.sum(own, axis=0, keepdims=True)
    scaled = (middle * gain_ref[...].astype(F32)).astype(BF16)
    scaled_ref[...] = scaled
    put_gate(
        own_ref,
        out_ref,
        jnp.dot(scaled, weight_ref[...], preferred_element_type=F32),
        jnp.sum(middle * middle, axis=1, keepdims=True),
    )


def put_gate(own_ref, out_ref, gate, square):
    columns, end = gate.shape[1], own_ref.shape[1] - 128
    own_ref[:, :columns] = gate
    own_ref[:, end:] = jnp.broadcast_to(square, (gate.shape[0], 128))
    out_ref[:, :columns] = gate.astype(BF16)
    put_sums(out_ref, end, square)


def up_kernel(scaled_ref, weight_ref, own_ref, out_ref):
    up = jnp.dot(scaled_ref[...], weight_ref[...], preferred_element_type=F32)
    own_ref[...] = up
    out_ref[...] = up.astype(BF16)


def merge_kernel(first_ref, second_ref, own_ref, out_ref):
    total = first_ref[...] + second_ref[...].astype(F32)
    own_ref[...] = total
    out_ref[...] = total.astype(BF16)


def merge_sums_kernel(columns, first_ref, second_ref, own_ref, out_ref):
    end = own_ref.shape[1] - 128
    put_gate(
        own_ref,
        out_ref,
        first_ref[:, :columns] + second_ref[:, :columns].astype(F32),
        first_ref[:, end : end + 1] + get_sums(second_ref, end),
    )


def contract_kernel(
    first_gate_ref, second_gate_ref, first_up_ref, second_up_ref, weight_ref, out_ref
):
    end = first_gate_ref.shape[1] - 128
    columns = weight_ref.shape[0]
    square = first_gate_ref[:, end : end + 1] + get_sums(second_gate_ref, end)
    factor = lax.rsqrt(square / D + 1e-06)
    gate = first_gate_ref[:, :columns] + second_gate_ref[:, :columns].astype(F32)
    gate = gate * factor
    up = (first_up_ref[...] + second_up_ref[...].astype(F32)) * factor
    hidden = (gate / (1.0 + jnp.exp(-gate)) * up).astype(BF16)
    total = jnp.dot(hidden, weight_ref[...], preferred_element_type=F32)
    slots = out_ref.shape[1]
    for owner in range(out_ref.shape[0]):
        out_ref[owner] = total[owner * slots : (owner + 1) * slots]


def exchange(array, first, second, wide, narrow):
    pairs = [
        (w * narrow + n, (w ^ (second if n % 2 else first)) * narrow + n)
        for w in range(wide)
        for n in range(narrow)
    ]
    return lax.ppermute(array, ("wide", "narrow"), pairs)


def exchange_groups(size):
    bits = size.bit_length() - 1
    groups = [[1]] if bits else []
    for bit in range(1, bits, 2):
        groups.append([part << bit for part in range(1, 4 if bit + 1 < bits else 2)])
    return groups


def swap(array, axis, distance, size):
    return lax.ppermute(array, axis, [(i, i ^ distance) for i in range(size)])


def shards(
    wide,
    narrow,
    residual_in,
    query_nope,
    query_rope,
    absorb_key,
    absorb_value,
    latent_cache,
    cache_lengths,
    slot_rows,
    out_proj,
    norm_gain,
    gate_weight,
    up_weight,
    down_weight,
):
    slots, heads, head_size = query_nope.shape
    rope = query_rope.shape[2]
    features = out_proj.shape[1]
    rows = slot_rows.shape[0]
    per_block = out_proj.shape[0] // head_size
    blocks = heads // per_block
    group = lax.axis_index("wide").astype(jnp.int32)
    scale = 1.0 / math.sqrt(head_size + rope)

    packed = call(
        pack_kernel,
        pltpu.VMEM((wide, slots, heads + heads // 2, head_size), BF16),
        [SMEM, HBM, HBM],
        "pack",
        [
            pltpu.VMEM(query_nope.shape, BF16),
            pltpu.VMEM(query_rope.shape, BF16),
            pltpu.SemaphoreType.DMA((2,)),
        ],
        flops=PACK,
    )(group[None], far(query_nope), far(query_rope))
    queries = lax.all_to_all(packed, "wide", 0, 0, tiled=True)
    cache = jnp.swapaxes(latent_cache, 1, 2)
    heads_out = call(
        functools.partial(attend_kernel, narrow, blocks, scale),
        pltpu.VMEM((wide * narrow, slots * per_block, head_size), BF16),
        [SMEM, SMEM, SMEM, VMEM, VMEM, VMEM, VMEM],
        "attend",
        flops=ATTEND,
    )(
        group[None],
        slot_rows,
        cache_lengths,
        queries,
        near(absorb_key),
        near(cache),
        near(absorb_value),
    )
    received = lax.all_to_all(heads_out, ("wide", "narrow"), 0, 0, tiled=True)
    total, summed = call(
        functools.partial(project_kernel, narrow, blocks),
        (pltpu.VMEM((rows, features), F32), pltpu.VMEM((rows, features), BF16)),
        [SMEM, SMEM, VMEM, VMEM, VMEM],
        "project",
        flops=PROJECT,
    )(slot_rows, group[None], received, residual_in, out_proj)
    groups = exchange_groups(wide)
    for index, distances in enumerate(groups):
        others = [
            exchange(summed, first, second, wide, narrow)
            for first, second in zip(distances, distances[::-1])
        ]
        if index + 1 < len(groups):
            for other in others:
                total = total + other.astype(F32)
            summed = total.astype(BF16)
    columns = gate_weight.shape[1]
    padded = -(-columns // 128) * 128
    gate_shapes = (pltpu.VMEM((rows, padded + 128), F32), pltpu.VMEM((rows, padded + 256), BF16))
    up_shapes = (pltpu.VMEM((rows, columns), F32), pltpu.VMEM((rows, columns), BF16))
    middle, scaled, gate, gate_sent = call(
        gate_kernel,
        (pltpu.VMEM((slots, features), F32), pltpu.VMEM((rows, features), BF16)) + gate_shapes,
        [SMEM] + [VMEM] * (3 + len(others)),
        "gate",
        flops=EXPAND // 2,
    )(group[None], norm_gain[None, :], gate_weight, total, *others)
    up, up_sent = call(up_kernel, up_shapes, [VMEM] * 2, "up", flops=EXPAND // 2)(
        scaled, up_weight
    )
    distance = narrow // 2
    while distance:
        other_gate = swap(gate_sent, "narrow", distance, narrow)
        other_up = swap(up_sent, "narrow", distance, narrow)
        distance //= 2
        if distance:
            gate, gate_sent = call(
                functools.partial(merge_sums_kernel, columns),
                gate_shapes,
                [VMEM] * 2,
                "merge_gate",
                flops=MERGE // 4,
            )(gate, other_gate)
            up, up_sent = call(
                merge_kernel, up_shapes, [VMEM] * 2, "merge_up", flops=MERGE // 4
            )(up, other_up)
    down = call(
        contract_kernel,
        pltpu.VMEM((wide, slots, features), F32),
        [VMEM] * 5,
        "contract",
        flops=CONTRACT,
    )(gate, other_gate, up, other_up, down_weight)
    total = jnp.sum(lax.all_to_all(down, "wide", 0, 0, tiled=True), axis=0)
    return (middle + total).astype(BF16)


def solution(mesh):
    in_specs = (
        P("wide", "narrow"),
        P("wide", "narrow", None),
        P("wide", "narrow", None),
        P("narrow", None, None),
        P("narrow", None, None),
        P("wide", None, None),
        P("wide"),
        P(),
        P("wide", "narrow"),
        P("narrow"),
        P("narrow", "wide"),
        P("narrow", "wide"),
        P("wide", "narrow"),
    )
    out_specs = P("wide", "narrow")
    body = functools.partial(shards, mesh.shape["wide"], mesh.shape["narrow"])
    return jax.shard_map(body, mesh=mesh, in_specs=in_specs, out_specs=out_specs, check_vma=False)
```

```python
import functools
import math

import jax
import jax.numpy as jnp
from jax import lax
from jax.experimental import pallas as pl
from jax.experimental.pallas import tpu as pltpu
from jax.sharding import PartitionSpec as P

D = 7168
BF16 = jnp.bfloat16
F32 = jnp.float32
VMEM = pl.BlockSpec(memory_space=pltpu.VMEM)
SMEM = pl.BlockSpec(memory_space=pltpu.SMEM)
HBM = pl.BlockSpec(memory_space=pltpu.HBM)
NT = (((1,), (1,)), ((), ()))


PACK = 10 * 10**9
ATTEND = 15 * 10**9
PROJECT = 12 * 10**9
EXPAND = 4 * 10**9
MERGE = 4 * 10**9
CONTRACT = 4 * 10**9


def near(array):
    return pltpu.with_memory_space_constraint(array, pltpu.VMEM)


def far(array):
    return pltpu.with_memory_space_constraint(array, pltpu.HBM)


def call(kernel, out_shape, in_specs, name, scratch=(), flops=0):
    return pl.pallas_call(
        kernel,
        out_shape=out_shape,
        scratch_shapes=scratch,
        cost_estimate=pl.CostEstimate(flops=flops, transcendentals=0, bytes_accessed=0),
        in_specs=in_specs,
        out_specs=jax.tree.map(lambda _: VMEM, out_shape),
        compiler_params=pltpu.CompilerParams(vmem_limit_bytes=8 * 1024 * 1024),
        name=name,
    )


def pack_kernel(group_ref, nope_hbm, rope_hbm, out_ref, nope_ref, rope_ref, sems):
    copies = [
        pltpu.make_async_copy(nope_hbm, nope_ref, sems.at[0]),
        pltpu.make_async_copy(rope_hbm, rope_ref, sems.at[1]),
    ]
    for copy in copies:
        copy.start()
    heads = nope_ref.shape[1]
    for copy in copies:
        copy.wait()
    pairs = jnp.concatenate([rope_ref[:, : heads // 2], rope_ref[:, heads // 2 :]], axis=2)
    row = jnp.concatenate([nope_ref[...], pairs], axis=1)
    for target in range(out_ref.shape[0]):
        out_ref[target] = row


def attend_kernel(
    narrow,
    blocks,
    scale,
    group_ref,
    rows_ref,
    lengths_ref,
    query_ref,
    key_ref,
    cache_ref,
    value_ref,
    out_ref,
):
    slots, latent = cache_ref.shape[0], value_ref.shape[1]
    heads, head_size = key_ref.shape[0], key_ref.shape[1]
    rope = cache_ref.shape[1] - latent
    span = cache_ref.shape[2]
    group = group_ref[0]
    queries = []
    for slot in range(slots):
        row = rows_ref[group * slots + slot]
        queries.append(query_ref[row // slots, row % slots])
    nope = jnp.concatenate([query[:heads] for query in queries], axis=0)
    ropes = [
        jnp.concatenate([query[heads:, :rope], query[heads:, rope:]], axis=0) for query in queries
    ]
    own_head = lax.broadcasted_iota(jnp.int32, (slots * heads, 1), 0) % heads
    total = jnp.zeros((slots * heads, latent), F32)
    for head in range(heads):
        term = jnp.dot(nope, key_ref[head], preferred_element_type=F32)
        total = jnp.where(own_head == head, term, total)
    query_latent = total.astype(BF16)
    parts = [slice(slot * heads, (slot + 1) * heads) for slot in range(slots)]
    scores = [
        jnp.dot(query_latent[part], cache_ref[slot, :latent, :], preferred_element_type=F32)
        + jnp.dot(
            ropes[slot],
            cache_ref[slot, latent:, :],
            preferred_element_type=F32,
        )
        for slot, part in enumerate(parts)
    ]
    probs = []
    for slot in range(slots):
        live = lax.broadcasted_iota(jnp.int32, (1, span), 1) < lengths_ref[slot]
        masked = jnp.where(live, scores[slot] * scale, -jnp.inf)
        weights = jnp.exp(masked - jnp.max(masked, axis=1, keepdims=True))
        probs.append((weights / jnp.sum(weights, axis=1, keepdims=True)).astype(BF16))
    context = jnp.concatenate(
        [
            lax.dot_general(
                probs[slot], cache_ref[slot, :latent, :], NT, preferred_element_type=F32
            ).astype(BF16)
            for slot in range(slots)
        ],
        axis=0,
    )
    total = jnp.zeros((slots * heads, head_size), F32)
    for head in range(heads):
        term = jnp.dot(context, value_ref[head], preferred_element_type=F32)
        total = jnp.where(own_head == head, term, total)
    heads_out = total.astype(BF16)
    per_block = heads // blocks
    pieces = []
    for block in range(blocks):
        low = block * per_block
        pieces.append(
            jnp.concatenate(
                [
                    heads_out[slot * heads + low : slot * heads + low + per_block]
                    for slot in range(slots)
                ],
                axis=0,
            )
        )
    for target in range(out_ref.shape[0]):
        out_ref[target] = pieces[(target // narrow) % blocks]


def project_kernel(
    narrow, blocks, rows_ref, group_ref, heads_ref, residual_ref, weight_ref, own_ref, out_ref
):
    wide = heads_ref.shape[0] // narrow
    slots = residual_ref.shape[0]
    rows = wide * slots
    per_block = heads_ref.shape[1] // slots
    head_size = heads_ref.shape[2]
    group = group_ref[0]
    holder = group // blocks
    received = jnp.concatenate(
        [heads_ref[source * narrow + holder] for source in range(wide)], axis=0
    )
    count = rows * per_block
    column = lax.broadcasted_iota(jnp.int32, (1, count), 1)
    column_row = jnp.zeros((1, count), jnp.int32)
    for slot in range(rows):
        column_row = jnp.where(column // per_block == slot, rows_ref[slot], column_row)
    wanted = column_row + rows * (column % per_block)
    position = lax.broadcasted_iota(jnp.int32, (count, count), 0)
    select = jnp.where(position == wanted, 1.0, 0.0).astype(BF16)
    ordered = jnp.dot(select, received, preferred_element_type=F32).astype(BF16)
    flat = jnp.concatenate(
        [ordered[head * rows : (head + 1) * rows] for head in range(per_block)], axis=1
    )
    total = jnp.dot(flat, weight_ref[...], preferred_element_type=F32)
    row = lax.broadcasted_iota(jnp.int32, (rows, 1), 0)
    for slot in range(slots):
        own = residual_ref[slot : slot + 1, :].astype(F32)
        total = total + jnp.where(row == group * slots + slot, own, 0.0)
    own_ref[...] = total
    out_ref[...] = total.astype(BF16)


def split_sum(value):
    high = value.astype(BF16)
    low = (value - high.astype(F32)).astype(BF16)
    return high, low


def put_sums(out_ref, start, value):
    high, low = split_sum(value)
    shape = (value.shape[0], 128)
    out_ref[:, start : start + 128] = jnp.broadcast_to(high, shape)
    out_ref[:, start + 128 : start + 256] = jnp.broadcast_to(low, shape)


def get_sums(ref, start):
    return ref[:, start : start + 1].astype(F32) + ref[:, start + 128 : start + 129].astype(F32)


def put_terms(own_ref, out_ref, gate, up, square):
    columns = gate.shape[1]
    padded = -(-columns // 128) * 128
    for side, terms in enumerate((gate, up)):
        place = slice(side * padded, side * padded + columns)
        own_ref[:, place] = terms
        out_ref[:, place] = terms.astype(BF16)
    if square is not None:
        own_ref[:, 2 * padded :] = jnp.broadcast_to(square, (gate.shape[0], 128))
        put_sums(out_ref, 2 * padded, square)


def get_terms(columns, own_ref, arrived_ref, with_square):
    padded = -(-columns // 128) * 128
    gate, up = (
        own_ref[:, start : start + columns] + arrived_ref[:, start : start + columns].astype(F32)
        for start in (0, padded)
    )
    square = None
    if with_square:
        square = own_ref[:, 2 * padded : 2 * padded + 1] + get_sums(arrived_ref, 2 * padded)
    return gate, up, square


def expand_first_kernel(cut, group_ref, gain_ref, gate_ref, up_ref, *refs):
    parts, (middle_ref, scaled_ref, own_ref, out_ref) = refs[:-4], refs[-4:]
    middle = parts[0][...].astype(F32)
    for part in parts[1:]:
        middle = middle + part[...].astype(F32)
    slots = middle_ref.shape[0]
    row = lax.broadcasted_iota(jnp.int32, (middle.shape[0], 1), 0)
    for slot in range(slots):
        own = jnp.where(row == group_ref[0] * slots + slot, middle, 0.0)
        middle_ref[slot : slot + 1] = jnp.sum(own, axis=0, keepdims=True)
    scaled = (middle * gain_ref[...].astype(F32)).astype(BF16)
    scaled_ref[...] = scaled
    put_terms(
        own_ref,
        out_ref,
        jnp.dot(scaled, gate_ref[:, :cut], preferred_element_type=F32),
        jnp.dot(scaled, up_ref[:, :cut], preferred_element_type=F32),
        jnp.sum(middle * middle, axis=1, keepdims=True),
    )


def expand_second_kernel(cut, scaled_ref, gate_ref, up_ref, own_ref, out_ref):
    scaled = scaled_ref[...]
    put_terms(
        own_ref,
        out_ref,
        jnp.dot(scaled, gate_ref[:, cut:], preferred_element_type=F32),
        jnp.dot(scaled, up_ref[:, cut:], preferred_element_type=F32),
        None,
    )


def merge_kernel(columns, with_square, first_ref, second_ref, own_ref, out_ref):
    put_terms(own_ref, out_ref, *get_terms(columns, first_ref, second_ref, with_square))


def activated(gate, up, factor):
    gate = gate * factor
    return (gate / (1.0 + jnp.exp(-gate)) * (up * factor)).astype(BF16)


def contract_first_kernel(cut, own_ref, arrived_ref, weight_ref, factor_ref, out_ref):
    gate, up, square = get_terms(cut, own_ref, arrived_ref, True)
    factor = lax.rsqrt(square / D + 1e-06)
    factor_ref[...] = jnp.broadcast_to(factor, factor_ref.shape)
    out_ref[...] = jnp.dot(
        activated(gate, up, factor), weight_ref[:cut, :], preferred_element_type=F32
    )


def contract_second_kernel(
    cut, own_ref, arrived_ref, weight_ref, factor_ref, partial_ref, out_ref
):
    gate, up, _ = get_terms(weight_ref.shape[0] - cut, own_ref, arrived_ref, False)
    total = partial_ref[...] + jnp.dot(
        activated(gate, up, factor_ref[:, :1]), weight_ref[cut:, :], preferred_element_type=F32
    )
    slots = out_ref.shape[1]
    for owner in range(out_ref.shape[0]):
        out_ref[owner] = total[owner * slots : (owner + 1) * slots]


def exchange(array, first, second, wide, narrow):
    pairs = [
        (w * narrow + n, (w ^ (second if n % 2 else first)) * narrow + n)
        for w in range(wide)
        for n in range(narrow)
    ]
    return lax.ppermute(array, ("wide", "narrow"), pairs)


def exchange_groups(size):
    bits = size.bit_length() - 1
    groups = [[1]] if bits else []
    for bit in range(1, bits, 2):
        groups.append([part << bit for part in range(1, 4 if bit + 1 < bits else 2)])
    return groups


def swap(array, axis, distance, size):
    return lax.ppermute(array, axis, [(i, i ^ distance) for i in range(size)])


def shards(
    wide,
    narrow,
    residual_in,
    query_nope,
    query_rope,
    absorb_key,
    absorb_value,
    latent_cache,
    cache_lengths,
    slot_rows,
    out_proj,
    norm_gain,
    gate_weight,
    up_weight,
    down_weight,
):
    slots, heads, head_size = query_nope.shape
    rope = query_rope.shape[2]
    features = out_proj.shape[1]
    rows = slot_rows.shape[0]
    per_block = out_proj.shape[0] // head_size
    blocks = heads // per_block
    group = lax.axis_index("wide").astype(jnp.int32)
    scale = 1.0 / math.sqrt(head_size + rope)

    packed = call(
        pack_kernel,
        pltpu.VMEM((wide, slots, heads + heads // 2, head_size), BF16),
        [SMEM, HBM, HBM],
        "pack",
        [
            pltpu.VMEM(query_nope.shape, BF16),
            pltpu.VMEM(query_rope.shape, BF16),
            pltpu.SemaphoreType.DMA((2,)),
        ],
        flops=PACK,
    )(group[None], far(query_nope), far(query_rope))
    queries = lax.all_to_all(packed, "wide", 0, 0, tiled=True)
    cache = jnp.swapaxes(latent_cache, 1, 2)
    heads_out = call(
        functools.partial(attend_kernel, narrow, blocks, scale),
        pltpu.VMEM((wide * narrow, slots * per_block, head_size), BF16),
        [SMEM, SMEM, SMEM, VMEM, VMEM, VMEM, VMEM],
        "attend",
        flops=ATTEND,
    )(
        group[None],
        slot_rows,
        cache_lengths,
        queries,
        near(absorb_key),
        near(cache),
        near(absorb_value),
    )
    received = lax.all_to_all(heads_out, ("wide", "narrow"), 0, 0, tiled=True)
    total, summed = call(
        functools.partial(project_kernel, narrow, blocks),
        (pltpu.VMEM((rows, features), F32), pltpu.VMEM((rows, features), BF16)),
        [SMEM, SMEM, VMEM, VMEM, VMEM],
        "project",
        flops=PROJECT,
    )(slot_rows, group[None], received, residual_in, out_proj)
    groups = exchange_groups(wide)
    for index, distances in enumerate(groups):
        others = [
            exchange(summed, first, second, wide, narrow)
            for first, second in zip(distances, distances[::-1])
        ]
        if index + 1 < len(groups):
            for other in others:
                total = total + other.astype(F32)
            summed = total.astype(BF16)
    columns = gate_weight.shape[1]
    cut = -(-2 * columns // 768) * 256
    halves = [(cut, 128, 256), (columns - cut, 0, 0)]
    shapes = []
    for size, kept, sent in halves:
        width = -(-size // 128) * 256
        shapes.append((pltpu.VMEM((rows, width + kept), F32), pltpu.VMEM((rows, width + sent), BF16)))
    middle, scaled, own, terms = call(
        functools.partial(expand_first_kernel, cut),
        (pltpu.VMEM((slots, features), F32), pltpu.VMEM((rows, features), BF16)) + shapes[0],
        [SMEM] + [VMEM] * (4 + len(others)),
        "expand_first",
        flops=EXPAND // 2,
    )(group[None], norm_gain[None, :], gate_weight, up_weight, total, *others)
    first = (own, terms)
    second = call(
        functools.partial(expand_second_kernel, cut),
        shapes[1],
        [VMEM] * 3,
        "expand_second",
        flops=EXPAND // 2,
    )(scaled, gate_weight, up_weight)
    distance = narrow // 2
    while distance:
        arrived = [swap(half[1], "narrow", distance, narrow) for half in (first, second)]
        distance //= 2
        if distance:
            first, second = (
                call(
                    functools.partial(merge_kernel, size, kept > 0),
                    shape,
                    [VMEM] * 2,
                    "merge",
                    flops=MERGE // 4,
                )(half[0], other)
                for (size, kept, _), shape, half, other in zip(
                    halves, shapes, (first, second), arrived
                )
            )
    factor, partial = call(
        functools.partial(contract_first_kernel, cut),
        (pltpu.VMEM((rows, 128), F32), pltpu.VMEM((rows, features), F32)),
        [VMEM] * 3,
        "contract_first",
        flops=CONTRACT // 4,
    )(first[0], arrived[0], down_weight)
    down = call(
        functools.partial(contract_second_kernel, cut),
        pltpu.VMEM((wide, slots, features), F32),
        [VMEM] * 5,
        "contract_second",
        flops=CONTRACT,
    )(second[0], arrived[1], down_weight, factor, partial)
    total = jnp.sum(lax.all_to_all(down, "wide", 0, 0, tiled=True), axis=0)
    return (middle + total).astype(BF16)


def solution(mesh):
    in_specs = (
        P("wide", "narrow"),
        P("wide", "narrow", None),
        P("wide", "narrow", None),
        P("narrow", None, None),
        P("narrow", None, None),
        P("wide", None, None),
        P("wide"),
        P(),
        P("wide", "narrow"),
        P("narrow"),
        P("narrow", "wide"),
        P("narrow", "wide"),
        P("wide", "narrow"),
    )
    out_specs = P("wide", "narrow")
    body = functools.partial(shards, mesh.shape["wide"], mesh.shape["narrow"])
    return jax.shard_map(body, mesh=mesh, in_specs=in_specs, out_specs=out_specs, check_vma=False)
```

```python
import functools
import math

import jax
import jax.numpy as jnp
from jax import lax
from jax.experimental import pallas as pl
from jax.experimental.pallas import tpu as pltpu
from jax.sharding import PartitionSpec as P

D = 7168
BF16 = jnp.bfloat16
F32 = jnp.float32
VMEM = pl.BlockSpec(memory_space=pltpu.VMEM)
SMEM = pl.BlockSpec(memory_space=pltpu.SMEM)
HBM = pl.BlockSpec(memory_space=pltpu.HBM)
NT = (((1,), (1,)), ((), ()))


PACK = 10 * 10**9
ATTEND = 15 * 10**9
PROJECT = 12 * 10**9
EXPAND = 4 * 10**9
MERGE = 4 * 10**9
CONTRACT = 4 * 10**9


def near(array):
    return pltpu.with_memory_space_constraint(array, pltpu.VMEM)


def far(array):
    return pltpu.with_memory_space_constraint(array, pltpu.HBM)


def call(kernel, out_shape, in_specs, name, scratch=(), flops=0):
    return pl.pallas_call(
        kernel,
        out_shape=out_shape,
        scratch_shapes=scratch,
        cost_estimate=pl.CostEstimate(flops=flops, transcendentals=0, bytes_accessed=0),
        in_specs=in_specs,
        out_specs=jax.tree.map(lambda _: VMEM, out_shape),
        compiler_params=pltpu.CompilerParams(vmem_limit_bytes=8 * 1024 * 1024),
        name=name,
    )


def pack_kernel(group_ref, nope_hbm, rope_hbm, out_ref, nope_ref, rope_ref, sems):
    copies = [
        pltpu.make_async_copy(nope_hbm, nope_ref, sems.at[0]),
        pltpu.make_async_copy(rope_hbm, rope_ref, sems.at[1]),
    ]
    for copy in copies:
        copy.start()
    heads = nope_ref.shape[1]
    for copy in copies:
        copy.wait()
    pairs = jnp.concatenate([rope_ref[:, : heads // 2], rope_ref[:, heads // 2 :]], axis=2)
    row = jnp.concatenate([nope_ref[...], pairs], axis=1)
    for target in range(out_ref.shape[0]):
        out_ref[target] = row


def attend_kernel(
    narrow,
    blocks,
    scale,
    group_ref,
    rows_ref,
    lengths_ref,
    query_ref,
    key_ref,
    cache_ref,
    value_ref,
    out_ref,
):
    slots, latent = cache_ref.shape[0], value_ref.shape[1]
    heads, head_size = key_ref.shape[0], key_ref.shape[1]
    rope = cache_ref.shape[1] - latent
    span = cache_ref.shape[2]
    group = group_ref[0]
    queries = []
    for slot in range(slots):
        row = rows_ref[group * slots + slot]
        queries.append(query_ref[row // slots, row % slots])
    nope = jnp.concatenate([query[:heads] for query in queries], axis=0)
    ropes = [
        jnp.concatenate([query[heads:, :rope], query[heads:, rope:]], axis=0) for query in queries
    ]
    own_head = lax.broadcasted_iota(jnp.int32, (slots * heads, 1), 0) % heads
    total = jnp.zeros((slots * heads, latent), F32)
    for head in range(heads):
        term = jnp.dot(nope, key_ref[head], preferred_element_type=F32)
        total = jnp.where(own_head == head, term, total)
    query_latent = total.astype(BF16)
    parts = [slice(slot * heads, (slot + 1) * heads) for slot in range(slots)]
    scores = [
        jnp.dot(query_latent[part], cache_ref[slot, :latent, :], preferred_element_type=F32)
        + jnp.dot(
            ropes[slot],
            cache_ref[slot, latent:, :],
            preferred_element_type=F32,
        )
        for slot, part in enumerate(parts)
    ]
    probs = []
    for slot in range(slots):
        live = lax.broadcasted_iota(jnp.int32, (1, span), 1) < lengths_ref[slot]
        masked = jnp.where(live, scores[slot] * scale, -jnp.inf)
        weights = jnp.exp(masked - jnp.max(masked, axis=1, keepdims=True))
        probs.append((weights / jnp.sum(weights, axis=1, keepdims=True)).astype(BF16))
    context = jnp.concatenate(
        [
            lax.dot_general(
                probs[slot], cache_ref[slot, :latent, :], NT, preferred_element_type=F32
            ).astype(BF16)
            for slot in range(slots)
        ],
        axis=0,
    )
    total = jnp.zeros((slots * heads, head_size), F32)
    for head in range(heads):
        term = jnp.dot(context, value_ref[head], preferred_element_type=F32)
        total = jnp.where(own_head == head, term, total)
    heads_out = total.astype(BF16)
    per_block = heads // blocks
    pieces = []
    for block in range(blocks):
        low = block * per_block
        pieces.append(
            jnp.concatenate(
                [
                    heads_out[slot * heads + low : slot * heads + low + per_block]
                    for slot in range(slots)
                ],
                axis=0,
            )
        )
    for target in range(out_ref.shape[0]):
        out_ref[target] = pieces[(target // narrow) % blocks]


def project_kernel(
    narrow, blocks, rows_ref, group_ref, heads_ref, residual_ref, weight_ref, own_ref, out_ref
):
    wide = heads_ref.shape[0] // narrow
    slots = residual_ref.shape[0]
    rows = wide * slots
    per_block = heads_ref.shape[1] // slots
    head_size = heads_ref.shape[2]
    group = group_ref[0]
    holder = group // blocks
    received = jnp.concatenate(
        [heads_ref[source * narrow + holder] for source in range(wide)], axis=0
    )
    count = rows * per_block
    column = lax.broadcasted_iota(jnp.int32, (1, count), 1)
    column_row = jnp.zeros((1, count), jnp.int32)
    for slot in range(rows):
        column_row = jnp.where(column // per_block == slot, rows_ref[slot], column_row)
    wanted = column_row + rows * (column % per_block)
    position = lax.broadcasted_iota(jnp.int32, (count, count), 0)
    select = jnp.where(position == wanted, 1.0, 0.0).astype(BF16)
    ordered = jnp.dot(select, received, preferred_element_type=F32).astype(BF16)
    flat = jnp.concatenate(
        [ordered[head * rows : (head + 1) * rows] for head in range(per_block)], axis=1
    )
    total = jnp.dot(flat, weight_ref[...], preferred_element_type=F32)
    row = lax.broadcasted_iota(jnp.int32, (rows, 1), 0)
    for slot in range(slots):
        own = residual_ref[slot : slot + 1, :].astype(F32)
        total = total + jnp.where(row == group * slots + slot, own, 0.0)
    own_ref[...] = total
    out_ref[...] = total.astype(BF16)


def split_sum(value):
    high = value.astype(BF16)
    low = (value - high.astype(F32)).astype(BF16)
    return high, low


def put_sums(out_ref, start, value):
    high, low = split_sum(value)
    shape = (value.shape[0], 128)
    out_ref[:, start : start + 128] = jnp.broadcast_to(high, shape)
    out_ref[:, start + 128 : start + 256] = jnp.broadcast_to(low, shape)


def get_sums(ref, start):
    return ref[:, start : start + 1].astype(F32) + ref[:, start + 128 : start + 129].astype(F32)


def put_terms(own_ref, out_ref, gate, up, square):
    columns = gate.shape[1]
    padded = -(-columns // 128) * 128
    for side, terms in enumerate((gate, up)):
        place = slice(side * padded, side * padded + columns)
        own_ref[:, place] = terms
        out_ref[:, place] = terms.astype(BF16)
    if square is not None:
        own_ref[:, 2 * padded :] = jnp.broadcast_to(square, (gate.shape[0], 128))
        put_sums(out_ref, 2 * padded, square)


def get_terms(columns, own_ref, arrived_ref, with_square):
    padded = -(-columns // 128) * 128
    gate, up = (
        own_ref[:, start : start + columns] + arrived_ref[:, start : start + columns].astype(F32)
        for start in (0, padded)
    )
    square = None
    if with_square:
        square = own_ref[:, 2 * padded : 2 * padded + 1] + get_sums(arrived_ref, 2 * padded)
    return gate, up, square


def expand_first_kernel(cut, group_ref, gain_ref, gate_ref, up_ref, *refs):
    parts, (middle_ref, scaled_ref, own_ref, out_ref) = refs[:-4], refs[-4:]
    middle = parts[0][...].astype(F32)
    for part in parts[1:]:
        middle = middle + part[...].astype(F32)
    slots = middle_ref.shape[0]
    row = lax.broadcasted_iota(jnp.int32, (middle.shape[0], 1), 0)
    for slot in range(slots):
        own = jnp.where(row == group_ref[0] * slots + slot, middle, 0.0)
        middle_ref[slot : slot + 1] = jnp.sum(own, axis=0, keepdims=True)
    scaled = (middle * gain_ref[...].astype(F32)).astype(BF16)
    scaled_ref[...] = scaled
    put_terms(
        own_ref,
        out_ref,
        jnp.dot(scaled, gate_ref[:, :cut], preferred_element_type=F32),
        jnp.dot(scaled, up_ref[:, :cut], preferred_element_type=F32),
        jnp.sum(middle * middle, axis=1, keepdims=True),
    )


def expand_second_kernel(cut, scaled_ref, gate_ref, up_ref, own_ref, out_ref):
    scaled = scaled_ref[...]
    put_terms(
        own_ref,
        out_ref,
        jnp.dot(scaled, gate_ref[:, cut:], preferred_element_type=F32),
        jnp.dot(scaled, up_ref[:, cut:], preferred_element_type=F32),
        None,
    )


def merge_kernel(columns, with_square, first_ref, second_ref, own_ref, out_ref):
    put_terms(own_ref, out_ref, *get_terms(columns, first_ref, second_ref, with_square))


def activated(gate, up, factor):
    gate = gate * factor
    return (gate / (1.0 + jnp.exp(-gate)) * (up * factor)).astype(BF16)


def contract_first_kernel(cut, own_ref, arrived_ref, weight_ref, factor_ref, out_ref):
    gate, up, square = get_terms(cut, own_ref, arrived_ref, True)
    factor = lax.rsqrt(square / D + 1e-06)
    factor_ref[...] = jnp.broadcast_to(factor, factor_ref.shape)
    out_ref[...] = jnp.dot(
        activated(gate, up, factor), weight_ref[:cut, :], preferred_element_type=F32
    )


def contract_second_kernel(
    cut, own_ref, arrived_ref, weight_ref, factor_ref, partial_ref, out_ref
):
    gate, up, _ = get_terms(weight_ref.shape[0] - cut, own_ref, arrived_ref, False)
    total = partial_ref[...] + jnp.dot(
        activated(gate, up, factor_ref[:, :1]), weight_ref[cut:, :], preferred_element_type=F32
    )
    slots = out_ref.shape[1]
    for owner in range(out_ref.shape[0]):
        out_ref[owner] = total[owner * slots : (owner + 1) * slots].astype(out_ref.dtype)


def exchange(array, first, second, wide, narrow):
    pairs = [
        (w * narrow + n, (w ^ (second if n % 2 else first)) * narrow + n)
        for w in range(wide)
        for n in range(narrow)
    ]
    return lax.ppermute(array, ("wide", "narrow"), pairs)


def exchange_groups(size):
    bits = size.bit_length() - 1
    groups = [[1]] if bits else []
    for bit in range(1, bits, 2):
        groups.append([part << bit for part in range(1, 4 if bit + 1 < bits else 2)])
    return groups


def swap(array, axis, distance, size):
    return lax.ppermute(array, axis, [(i, i ^ distance) for i in range(size)])


def shards(
    wide,
    narrow,
    residual_in,
    query_nope,
    query_rope,
    absorb_key,
    absorb_value,
    latent_cache,
    cache_lengths,
    slot_rows,
    out_proj,
    norm_gain,
    gate_weight,
    up_weight,
    down_weight,
):
    slots, heads, head_size = query_nope.shape
    rope = query_rope.shape[2]
    features = out_proj.shape[1]
    rows = slot_rows.shape[0]
    per_block = out_proj.shape[0] // head_size
    blocks = heads // per_block
    group = lax.axis_index("wide").astype(jnp.int32)
    scale = 1.0 / math.sqrt(head_size + rope)

    packed = call(
        pack_kernel,
        pltpu.VMEM((wide, slots, heads + heads // 2, head_size), BF16),
        [SMEM, HBM, HBM],
        "pack",
        [
            pltpu.VMEM(query_nope.shape, BF16),
            pltpu.VMEM(query_rope.shape, BF16),
            pltpu.SemaphoreType.DMA((2,)),
        ],
        flops=PACK,
    )(group[None], far(query_nope), far(query_rope))
    queries = lax.all_to_all(packed, "wide", 0, 0, tiled=True)
    cache = jnp.swapaxes(latent_cache, 1, 2)
    heads_out = call(
        functools.partial(attend_kernel, narrow, blocks, scale),
        pltpu.VMEM((wide * narrow, slots * per_block, head_size), BF16),
        [SMEM, SMEM, SMEM, VMEM, VMEM, VMEM, VMEM],
        "attend",
        flops=ATTEND,
    )(
        group[None],
        slot_rows,
        cache_lengths,
        queries,
        near(absorb_key),
        near(cache),
        near(absorb_value),
    )
    received = lax.all_to_all(heads_out, ("wide", "narrow"), 0, 0, tiled=True)
    total, summed = call(
        functools.partial(project_kernel, narrow, blocks),
        (pltpu.VMEM((rows, features), F32), pltpu.VMEM((rows, features), BF16)),
        [SMEM, SMEM, VMEM, VMEM, VMEM],
        "project",
        flops=PROJECT,
    )(slot_rows, group[None], received, residual_in, out_proj)
    groups = exchange_groups(wide)
    for index, distances in enumerate(groups):
        others = [
            exchange(summed, first, second, wide, narrow)
            for first, second in zip(distances, distances[::-1])
        ]
        if index + 1 < len(groups):
            for other in others:
                total = total + other.astype(F32)
            summed = total.astype(BF16)
    columns = gate_weight.shape[1]
    cut = -(-2 * columns // 768) * 256
    halves = [(cut, 128, 256), (columns - cut, 0, 0)]
    shapes = []
    for size, kept, sent in halves:
        width = -(-size // 128) * 256
        shapes.append((pltpu.VMEM((rows, width + kept), F32), pltpu.VMEM((rows, width + sent), BF16)))
    middle, scaled, own, terms = call(
        functools.partial(expand_first_kernel, cut),
        (pltpu.VMEM((slots, features), F32), pltpu.VMEM((rows, features), BF16)) + shapes[0],
        [SMEM] + [VMEM] * (4 + len(others)),
        "expand_first",
        flops=EXPAND // 2,
    )(group[None], norm_gain[None, :], gate_weight, up_weight, total, *others)
    first = (own, terms)
    second = call(
        functools.partial(expand_second_kernel, cut),
        shapes[1],
        [VMEM] * 3,
        "expand_second",
        flops=EXPAND // 2,
    )(scaled, gate_weight, up_weight)
    distance = narrow // 2
    while distance:
        arrived = [swap(half[1], "narrow", distance, narrow) for half in (first, second)]
        distance //= 2
        if distance:
            first, second = (
                call(
                    functools.partial(merge_kernel, size, kept > 0),
                    shape,
                    [VMEM] * 2,
                    "merge",
                    flops=MERGE // 4,
                )(half[0], other)
                for (size, kept, _), shape, half, other in zip(
                    halves, shapes, (first, second), arrived
                )
            )
    factor, partial = call(
        functools.partial(contract_first_kernel, cut),
        (pltpu.VMEM((rows, 128), F32), pltpu.VMEM((rows, features), F32)),
        [VMEM] * 3,
        "contract_first",
        flops=CONTRACT // 4,
    )(first[0], arrived[0], down_weight)
    down = call(
        functools.partial(contract_second_kernel, cut),
        pltpu.VMEM((wide, slots, features), BF16),
        [VMEM] * 5,
        "contract_second",
        flops=CONTRACT,
    )(second[0], arrived[1], down_weight, factor, partial)
    total = jnp.sum(lax.all_to_all(down, "wide", 0, 0, tiled=True).astype(F32), axis=0)
    return (middle + total).astype(BF16)


def solution(mesh):
    in_specs = (
        P("wide", "narrow"),
        P("wide", "narrow", None),
        P("wide", "narrow", None),
        P("narrow", None, None),
        P("narrow", None, None),
        P("wide", None, None),
        P("wide"),
        P(),
        P("wide", "narrow"),
        P("narrow"),
        P("narrow", "wide"),
        P("narrow", "wide"),
        P("wide", "narrow"),
    )
    out_specs = P("wide", "narrow")
    body = functools.partial(shards, mesh.shape["wide"], mesh.shape["narrow"])
    return jax.shard_map(body, mesh=mesh, in_specs=in_specs, out_specs=out_specs, check_vma=False)
```

```python
import functools
import math

import jax
import jax.numpy as jnp
from jax import lax
from jax.experimental import pallas as pl
from jax.experimental.pallas import tpu as pltpu
from jax.sharding import PartitionSpec as P

D = 7168
BF16 = jnp.bfloat16
F32 = jnp.float32
VMEM = pl.BlockSpec(memory_space=pltpu.VMEM)
SMEM = pl.BlockSpec(memory_space=pltpu.SMEM)
HBM = pl.BlockSpec(memory_space=pltpu.HBM)
NT = (((1,), (1,)), ((), ()))


PACK = 10 * 10**9
ATTEND = 15 * 10**9
PROJECT = 12 * 10**9
EXPAND = 4 * 10**9
MERGE = 4 * 10**9
CONTRACT = 4 * 10**9


def near(array):
    return pltpu.with_memory_space_constraint(array, pltpu.VMEM)


def far(array):
    return pltpu.with_memory_space_constraint(array, pltpu.HBM)


def call(kernel, out_shape, in_specs, name, scratch=(), flops=0):
    return pl.pallas_call(
        kernel,
        out_shape=out_shape,
        scratch_shapes=scratch,
        cost_estimate=pl.CostEstimate(flops=flops, transcendentals=0, bytes_accessed=0),
        in_specs=in_specs,
        out_specs=jax.tree.map(lambda _: VMEM, out_shape),
        compiler_params=pltpu.CompilerParams(vmem_limit_bytes=8 * 1024 * 1024),
        name=name,
    )


def pack_kernel(group_ref, nope_hbm, rope_hbm, out_ref, nope_ref, rope_ref, sems):
    copies = [
        pltpu.make_async_copy(nope_hbm, nope_ref, sems.at[0]),
        pltpu.make_async_copy(rope_hbm, rope_ref, sems.at[1]),
    ]
    for copy in copies:
        copy.start()
    heads = nope_ref.shape[1]
    for copy in copies:
        copy.wait()
    pairs = jnp.concatenate([rope_ref[:, : heads // 2], rope_ref[:, heads // 2 :]], axis=2)
    row = jnp.concatenate([nope_ref[...], pairs], axis=1)
    for target in range(out_ref.shape[0]):
        out_ref[target] = row


def place_rows(group, per_block, rows_ref, residual_ref, select_ref, spread_ref):
    rows, slots = spread_ref.shape[0], residual_ref.shape[0]
    count = select_ref.shape[0]
    column = lax.broadcasted_iota(jnp.int32, (1, count), 1)
    column_row = jnp.zeros((1, count), jnp.int32)
    for slot in range(rows):
        column_row = jnp.where(column // per_block == slot, rows_ref[slot], column_row)
    wanted = column_row + rows * (column % per_block)
    position = lax.broadcasted_iota(jnp.int32, (count, count), 0)
    select_ref[...] = jnp.where(position == wanted, 1.0, 0.0).astype(BF16)
    row = lax.broadcasted_iota(jnp.int32, (rows, 1), 0)
    spread = jnp.zeros(spread_ref.shape, F32)
    for slot in range(slots):
        own = residual_ref[slot : slot + 1, :].astype(F32)
        spread = jnp.where(row == group * slots + slot, own, spread)
    spread_ref[...] = spread


def attend_kernel(
    narrow,
    blocks,
    scale,
    group_ref,
    rows_ref,
    lengths_ref,
    query_ref,
    key_ref,
    cache_ref,
    value_ref,
    residual_ref,
    out_ref,
    select_ref,
    spread_ref,
):
    slots, latent = cache_ref.shape[0], value_ref.shape[1]
    heads, head_size = key_ref.shape[0], key_ref.shape[1]
    rope = cache_ref.shape[1] - latent
    span = cache_ref.shape[2]
    group = group_ref[0]
    place_rows(group, heads // blocks, rows_ref, residual_ref, select_ref, spread_ref)
    queries = []
    for slot in range(slots):
        row = rows_ref[group * slots + slot]
        queries.append(query_ref[row // slots, row % slots])
    nope = jnp.concatenate([query[:heads] for query in queries], axis=0)
    ropes = [
        jnp.concatenate([query[heads:, :rope], query[heads:, rope:]], axis=0) for query in queries
    ]
    own_head = lax.broadcasted_iota(jnp.int32, (slots * heads, 1), 0) % heads
    total = jnp.zeros((slots * heads, latent), F32)
    for head in range(heads):
        term = jnp.dot(nope, key_ref[head], preferred_element_type=F32)
        total = jnp.where(own_head == head, term, total)
    query_latent = total.astype(BF16)
    parts = [slice(slot * heads, (slot + 1) * heads) for slot in range(slots)]
    scores = [
        jnp.dot(query_latent[part], cache_ref[slot, :latent, :], preferred_element_type=F32)
        + jnp.dot(
            ropes[slot],
            cache_ref[slot, latent:, :],
            preferred_element_type=F32,
        )
        for slot, part in enumerate(parts)
    ]
    probs = []
    for slot in range(slots):
        live = lax.broadcasted_iota(jnp.int32, (1, span), 1) < lengths_ref[slot]
        masked = jnp.where(live, scores[slot] * scale, -jnp.inf)
        weights = jnp.exp(masked - jnp.max(masked, axis=1, keepdims=True))
        probs.append((weights / jnp.sum(weights, axis=1, keepdims=True)).astype(BF16))
    context = jnp.concatenate(
        [
            lax.dot_general(
                probs[slot], cache_ref[slot, :latent, :], NT, preferred_element_type=F32
            ).astype(BF16)
            for slot in range(slots)
        ],
        axis=0,
    )
    total = jnp.zeros((slots * heads, head_size), F32)
    for head in range(heads):
        term = jnp.dot(context, value_ref[head], preferred_element_type=F32)
        total = jnp.where(own_head == head, term, total)
    heads_out = total.astype(BF16)
    per_block = heads // blocks
    pieces = []
    for block in range(blocks):
        low = block * per_block
        pieces.append(
            jnp.concatenate(
                [
                    heads_out[slot * heads + low : slot * heads + low + per_block]
                    for slot in range(slots)
                ],
                axis=0,
            )
        )
    for target in range(out_ref.shape[0]):
        out_ref[target] = pieces[(target // narrow) % blocks]


def project_kernel(
    narrow, blocks, group_ref, heads_ref, select_ref, residual_ref, weight_ref, own_ref, out_ref
):
    wide = heads_ref.shape[0] // narrow
    rows = own_ref.shape[0]
    holder = group_ref[0] // blocks
    received = jnp.concatenate(
        [heads_ref[source * narrow + holder] for source in range(wide)], axis=0
    )
    ordered = jnp.dot(select_ref[...], received, preferred_element_type=F32).astype(BF16)
    flat = jnp.concatenate(
        [ordered[first : first + rows] for first in range(0, ordered.shape[0], rows)], axis=1
    )
    total = residual_ref[...] + jnp.dot(flat, weight_ref[...], preferred_element_type=F32)
    own_ref[...] = total
    out_ref[...] = total.astype(BF16)


def split_sum(value):
    high = value.astype(BF16)
    low = (value - high.astype(F32)).astype(BF16)
    return high, low


def put_sums(out_ref, start, value):
    high, low = split_sum(value)
    shape = (value.shape[0], 128)
    out_ref[:, start : start + 128] = jnp.broadcast_to(high, shape)
    out_ref[:, start + 128 : start + 256] = jnp.broadcast_to(low, shape)


def get_sums(ref, start):
    return ref[:, start : start + 1].astype(F32) + ref[:, start + 128 : start + 129].astype(F32)


def put_terms(own_ref, out_ref, gate, up, square):
    columns = gate.shape[1]
    padded = -(-columns // 128) * 128
    for side, terms in enumerate((gate, up)):
        place = slice(side * padded, side * padded + columns)
        own_ref[:, place] = terms
        out_ref[:, place] = terms.astype(BF16)
    if square is not None:
        own_ref[:, 2 * padded :] = jnp.broadcast_to(square, (gate.shape[0], 128))
        put_sums(out_ref, 2 * padded, square)


def get_terms(columns, own_ref, arrived_ref, with_square):
    padded = -(-columns // 128) * 128
    gate, up = (
        own_ref[:, start : start + columns] + arrived_ref[:, start : start + columns].astype(F32)
        for start in (0, padded)
    )
    square = None
    if with_square:
        square = own_ref[:, 2 * padded : 2 * padded + 1] + get_sums(arrived_ref, 2 * padded)
    return gate, up, square


def expand_first_kernel(cut, group_ref, gain_ref, gate_ref, up_ref, *refs):
    parts, (middle_ref, scaled_ref, own_ref, out_ref) = refs[:-4], refs[-4:]
    middle = parts[0][...].astype(F32)
    for part in parts[1:]:
        middle = middle + part[...].astype(F32)
    slots = middle_ref.shape[0]
    row = lax.broadcasted_iota(jnp.int32, (middle.shape[0], 1), 0)
    for slot in range(slots):
        own = jnp.where(row == group_ref[0] * slots + slot, middle, 0.0)
        middle_ref[slot : slot + 1] = jnp.sum(own, axis=0, keepdims=True)
    scaled = (middle * gain_ref[...].astype(F32)).astype(BF16)
    scaled_ref[...] = scaled
    put_terms(
        own_ref,
        out_ref,
        jnp.dot(scaled, gate_ref[:, :cut], preferred_element_type=F32),
        jnp.dot(scaled, up_ref[:, :cut], preferred_element_type=F32),
        jnp.sum(middle * middle, axis=1, keepdims=True),
    )


def expand_second_kernel(cut, scaled_ref, gate_ref, up_ref, own_ref, out_ref):
    scaled = scaled_ref[...]
    put_terms(
        own_ref,
        out_ref,
        jnp.dot(scaled, gate_ref[:, cut:], preferred_element_type=F32),
        jnp.dot(scaled, up_ref[:, cut:], preferred_element_type=F32),
        None,
    )


def merge_kernel(columns, with_square, first_ref, second_ref, own_ref, out_ref):
    put_terms(own_ref, out_ref, *get_terms(columns, first_ref, second_ref, with_square))


def activated(gate, up, factor):
    gate = gate * factor
    return (gate / (1.0 + jnp.exp(-gate)) * (up * factor)).astype(BF16)


def contract_first_kernel(cut, own_ref, arrived_ref, weight_ref, factor_ref, out_ref):
    gate, up, square = get_terms(cut, own_ref, arrived_ref, True)
    factor = lax.rsqrt(square / D + 1e-06)
    factor_ref[...] = jnp.broadcast_to(factor, factor_ref.shape)
    out_ref[...] = jnp.dot(
        activated(gate, up, factor), weight_ref[:cut, :], preferred_element_type=F32
    )


def contract_second_kernel(
    cut, own_ref, arrived_ref, weight_ref, factor_ref, partial_ref, out_ref
):
    gate, up, _ = get_terms(weight_ref.shape[0] - cut, own_ref, arrived_ref, False)
    total = partial_ref[...] + jnp.dot(
        activated(gate, up, factor_ref[:, :1]), weight_ref[cut:, :], preferred_element_type=F32
    )
    slots = out_ref.shape[1]
    for owner in range(out_ref.shape[0]):
        out_ref[owner] = total[owner * slots : (owner + 1) * slots].astype(out_ref.dtype)


def exchange(array, first, second, wide, narrow):
    pairs = [
        (w * narrow + n, (w ^ (second if n % 2 else first)) * narrow + n)
        for w in range(wide)
        for n in range(narrow)
    ]
    return lax.ppermute(array, ("wide", "narrow"), pairs)


def exchange_groups(size):
    bits = size.bit_length() - 1
    groups = [[1]] if bits else []
    for bit in range(1, bits, 2):
        groups.append([part << bit for part in range(1, 4 if bit + 1 < bits else 2)])
    return groups


def swap(array, axis, distance, size):
    return lax.ppermute(array, axis, [(i, i ^ distance) for i in range(size)])


def shards(
    wide,
    narrow,
    residual_in,
    query_nope,
    query_rope,
    absorb_key,
    absorb_value,
    latent_cache,
    cache_lengths,
    slot_rows,
    out_proj,
    norm_gain,
    gate_weight,
    up_weight,
    down_weight,
):
    slots, heads, head_size = query_nope.shape
    rope = query_rope.shape[2]
    features = out_proj.shape[1]
    rows = slot_rows.shape[0]
    per_block = out_proj.shape[0] // head_size
    blocks = heads // per_block
    group = lax.axis_index("wide").astype(jnp.int32)
    scale = 1.0 / math.sqrt(head_size + rope)

    packed = call(
        pack_kernel,
        pltpu.VMEM((wide, slots, heads + heads // 2, head_size), BF16),
        [SMEM, HBM, HBM],
        "pack",
        [
            pltpu.VMEM(query_nope.shape, BF16),
            pltpu.VMEM(query_rope.shape, BF16),
            pltpu.SemaphoreType.DMA((2,)),
        ],
        flops=PACK,
    )(group[None], far(query_nope), far(query_rope))
    queries = lax.all_to_all(packed, "wide", 0, 0, tiled=True)
    cache = jnp.swapaxes(latent_cache, 1, 2)
    heads_out, select, spread = call(
        functools.partial(attend_kernel, narrow, blocks, scale),
        (
            pltpu.VMEM((wide * narrow, slots * per_block, head_size), BF16),
            pltpu.VMEM((rows * per_block, rows * per_block), BF16),
            pltpu.VMEM((rows, features), F32),
        ),
        [SMEM, SMEM, SMEM] + [VMEM] * 5,
        "attend",
        flops=ATTEND,
    )(
        group[None],
        slot_rows,
        cache_lengths,
        queries,
        near(absorb_key),
        near(cache),
        near(absorb_value),
        residual_in,
    )
    received = lax.all_to_all(heads_out, ("wide", "narrow"), 0, 0, tiled=True)
    total, summed = call(
        functools.partial(project_kernel, narrow, blocks),
        (pltpu.VMEM((rows, features), F32), pltpu.VMEM((rows, features), BF16)),
        [SMEM] + [VMEM] * 4,
        "project",
        flops=PROJECT,
    )(group[None], received, select, spread, out_proj)
    groups = exchange_groups(wide)
    for index, distances in enumerate(groups):
        others = [
            exchange(summed, first, second, wide, narrow)
            for first, second in zip(distances, distances[::-1])
        ]
        if index + 1 < len(groups):
            for other in others:
                total = total + other.astype(F32)
            summed = total.astype(BF16)
    columns = gate_weight.shape[1]
    cut = -(-2 * columns // 768) * 256
    halves = [(cut, 128, 256), (columns - cut, 0, 0)]
    shapes = []
    for size, kept, sent in halves:
        width = -(-size // 128) * 256
        shapes.append((pltpu.VMEM((rows, width + kept), F32), pltpu.VMEM((rows, width + sent), BF16)))
    middle, scaled, own, terms = call(
        functools.partial(expand_first_kernel, cut),
        (pltpu.VMEM((slots, features), F32), pltpu.VMEM((rows, features), BF16)) + shapes[0],
        [SMEM] + [VMEM] * (4 + len(others)),
        "expand_first",
        flops=EXPAND // 2,
    )(group[None], norm_gain[None, :], gate_weight, up_weight, total, *others)
    first = (own, terms)
    second = call(
        functools.partial(expand_second_kernel, cut),
        shapes[1],
        [VMEM] * 3,
        "expand_second",
        flops=EXPAND // 2,
    )(scaled, gate_weight, up_weight)
    distance = narrow // 2
    while distance:
        arrived = [swap(half[1], "narrow", distance, narrow) for half in (first, second)]
        distance //= 2
        if distance:
            first, second = (
                call(
                    functools.partial(merge_kernel, size, kept > 0),
                    shape,
                    [VMEM] * 2,
                    "merge",
                    flops=MERGE // 4,
                )(half[0], other)
                for (size, kept, _), shape, half, other in zip(
                    halves, shapes, (first, second), arrived
                )
            )
    factor, partial = call(
        functools.partial(contract_first_kernel, cut),
        (pltpu.VMEM((rows, 128), F32), pltpu.VMEM((rows, features), F32)),
        [VMEM] * 3,
        "contract_first",
        flops=CONTRACT // 4,
    )(first[0], arrived[0], down_weight)
    down = call(
        functools.partial(contract_second_kernel, cut),
        pltpu.VMEM((wide, slots, features), BF16),
        [VMEM] * 5,
        "contract_second",
        flops=CONTRACT,
    )(second[0], arrived[1], down_weight, factor, partial)
    total = jnp.sum(lax.all_to_all(down, "wide", 0, 0, tiled=True).astype(F32), axis=0)
    return (middle + total).astype(BF16)


def solution(mesh):
    in_specs = (
        P("wide", "narrow"),
        P("wide", "narrow", None),
        P("wide", "narrow", None),
        P("narrow", None, None),
        P("narrow", None, None),
        P("wide", None, None),
        P("wide"),
        P(),
        P("wide", "narrow"),
        P("narrow"),
        P("narrow", "wide"),
        P("narrow", "wide"),
        P("wide", "narrow"),
    )
    out_specs = P("wide", "narrow")
    body = functools.partial(shards, mesh.shape["wide"], mesh.shape["narrow"])
    return jax.shard_map(body, mesh=mesh, in_specs=in_specs, out_specs=out_specs, check_vma=False)
```

```python
import functools
import math

import jax
import jax.numpy as jnp
from jax import lax
from jax.experimental import pallas as pl
from jax.experimental.pallas import tpu as pltpu
from jax.sharding import PartitionSpec as P

D = 7168
CHUNK = 512
BF16 = jnp.bfloat16
F32 = jnp.float32
VMEM = pl.BlockSpec(memory_space=pltpu.VMEM)
SMEM = pl.BlockSpec(memory_space=pltpu.SMEM)
HBM = pl.BlockSpec(memory_space=pltpu.HBM)
NT = (((1,), (1,)), ((), ()))


PACK = 10 * 10**9
ATTEND = 15 * 10**9
PROJECT = 12 * 10**9
EXPAND = 4 * 10**9
MERGE = 4 * 10**9
CONTRACT = 4 * 10**9


def near(array):
    return pltpu.with_memory_space_constraint(array, pltpu.VMEM)


def far(array):
    return pltpu.with_memory_space_constraint(array, pltpu.HBM)


def call(kernel, out_shape, in_specs, name, scratch=(), flops=0):
    return pl.pallas_call(
        kernel,
        out_shape=out_shape,
        scratch_shapes=scratch,
        cost_estimate=pl.CostEstimate(flops=flops, transcendentals=0, bytes_accessed=0),
        in_specs=in_specs,
        out_specs=jax.tree.map(lambda _: VMEM, out_shape),
        compiler_params=pltpu.CompilerParams(vmem_limit_bytes=8 * 1024 * 1024),
        name=name,
    )


def pack_kernel(group_ref, nope_hbm, rope_hbm, out_ref, nope_ref, rope_ref, sems):
    copies = [
        pltpu.make_async_copy(nope_hbm, nope_ref, sems.at[0]),
        pltpu.make_async_copy(rope_hbm, rope_ref, sems.at[1]),
    ]
    for copy in copies:
        copy.start()
    heads = nope_ref.shape[1]
    for copy in copies:
        copy.wait()
    pairs = jnp.concatenate([rope_ref[:, : heads // 2], rope_ref[:, heads // 2 :]], axis=2)
    row = jnp.concatenate([nope_ref[...], pairs], axis=1)
    for target in range(out_ref.shape[0]):
        out_ref[target] = row


def place_rows(group, per_block, rows_ref, residual_ref, select_ref, spread_ref):
    rows, slots = spread_ref.shape[0], residual_ref.shape[0]
    count = select_ref.shape[0]
    column = lax.broadcasted_iota(jnp.int32, (1, count), 1)
    column_row = jnp.zeros((1, count), jnp.int32)
    for slot in range(rows):
        column_row = jnp.where(column // per_block == slot, rows_ref[slot], column_row)
    wanted = column_row + rows * (column % per_block)
    position = lax.broadcasted_iota(jnp.int32, (count, count), 0)
    select_ref[...] = jnp.where(position == wanted, 1.0, 0.0).astype(BF16)
    row = lax.broadcasted_iota(jnp.int32, (rows, 1), 0)
    spread = jnp.zeros(spread_ref.shape, F32)
    for slot in range(slots):
        own = residual_ref[slot : slot + 1, :].astype(F32)
        spread = jnp.where(row == group * slots + slot, own, spread)
    spread_ref[...] = spread


def attend_kernel(
    narrow,
    blocks,
    scale,
    group_ref,
    rows_ref,
    lengths_ref,
    query_ref,
    key_ref,
    cache_ref,
    value_ref,
    residual_ref,
    out_ref,
    select_ref,
    spread_ref,
):
    slots, latent = cache_ref.shape[0], value_ref.shape[1]
    heads, head_size = key_ref.shape[0], key_ref.shape[1]
    rope = cache_ref.shape[1] - latent
    span = cache_ref.shape[2]
    group = group_ref[0]
    place_rows(group, heads // blocks, rows_ref, residual_ref, select_ref, spread_ref)
    queries = []
    for slot in range(slots):
        row = rows_ref[group * slots + slot]
        queries.append(query_ref[row // slots, row % slots])
    nope = jnp.concatenate([query[:heads] for query in queries], axis=0)
    ropes = [
        jnp.concatenate([query[heads:, :rope], query[heads:, rope:]], axis=0) for query in queries
    ]
    own_head = lax.broadcasted_iota(jnp.int32, (slots * heads, 1), 0) % heads
    total = jnp.zeros((slots * heads, latent), F32)
    for head in range(heads):
        term = jnp.dot(nope, key_ref[head], preferred_element_type=F32)
        total = jnp.where(own_head == head, term, total)
    query_latent = total.astype(BF16)
    parts = [slice(slot * heads, (slot + 1) * heads) for slot in range(slots)]
    scores = [
        jnp.dot(query_latent[part], cache_ref[slot, :latent, :], preferred_element_type=F32)
        + jnp.dot(
            ropes[slot],
            cache_ref[slot, latent:, :],
            preferred_element_type=F32,
        )
        for slot, part in enumerate(parts)
    ]
    probs = []
    for slot in range(slots):
        live = lax.broadcasted_iota(jnp.int32, (1, span), 1) < lengths_ref[slot]
        masked = jnp.where(live, scores[slot] * scale, -jnp.inf)
        weights = jnp.exp(masked - jnp.max(masked, axis=1, keepdims=True))
        probs.append((weights / jnp.sum(weights, axis=1, keepdims=True)).astype(BF16))
    context = jnp.concatenate(
        [
            lax.dot_general(
                probs[slot], cache_ref[slot, :latent, :], NT, preferred_element_type=F32
            ).astype(BF16)
            for slot in range(slots)
        ],
        axis=0,
    )
    total = jnp.zeros((slots * heads, head_size), F32)
    for head in range(heads):
        term = jnp.dot(context, value_ref[head], preferred_element_type=F32)
        total = jnp.where(own_head == head, term, total)
    heads_out = total.astype(BF16)
    per_block = heads // blocks
    pieces = []
    for block in range(blocks):
        low = block * per_block
        pieces.append(
            jnp.concatenate(
                [
                    heads_out[slot * heads + low : slot * heads + low + per_block]
                    for slot in range(slots)
                ],
                axis=0,
            )
        )
    for target in range(out_ref.shape[0]):
        out_ref[target] = pieces[(target // narrow) % blocks]


def project_kernel(
    narrow, blocks, group_ref, heads_ref, select_ref, residual_ref, weight_ref, own_ref, out_ref
):
    wide = heads_ref.shape[0] // narrow
    rows = own_ref.shape[0]
    holder = group_ref[0] // blocks
    received = jnp.concatenate(
        [heads_ref[source * narrow + holder] for source in range(wide)], axis=0
    )
    ordered = jnp.dot(select_ref[...], received, preferred_element_type=F32).astype(BF16)
    flat = jnp.concatenate(
        [ordered[first : first + rows] for first in range(0, ordered.shape[0], rows)], axis=1
    )
    total = residual_ref[...] + jnp.dot(flat, weight_ref[...], preferred_element_type=F32)
    own_ref[...] = total
    out_ref[...] = total.astype(BF16)


def split_sum(value):
    high = value.astype(BF16)
    low = (value - high.astype(F32)).astype(BF16)
    return high, low


def put_sums(out_ref, start, value):
    high, low = split_sum(value)
    shape = (value.shape[0], 128)
    out_ref[:, start : start + 128] = jnp.broadcast_to(high, shape)
    out_ref[:, start + 128 : start + 256] = jnp.broadcast_to(low, shape)


def get_sums(ref, start):
    return ref[:, start : start + 1].astype(F32) + ref[:, start + 128 : start + 129].astype(F32)


def put_terms(own_ref, out_ref, gate, up, square):
    columns = gate.shape[1]
    padded = -(-columns // 128) * 128
    for side, terms in enumerate((gate, up)):
        place = slice(side * padded, side * padded + columns)
        own_ref[:, place] = terms
        out_ref[:, place] = terms.astype(BF16)
    if square is not None:
        own_ref[:, 2 * padded :] = jnp.broadcast_to(square, (gate.shape[0], 128))
        put_sums(out_ref, 2 * padded, square)


def get_terms(columns, own_ref, arrived_ref, with_square):
    padded = -(-columns // 128) * 128
    gate, up = (
        own_ref[:, start : start + columns] + arrived_ref[:, start : start + columns].astype(F32)
        for start in (0, padded)
    )
    square = None
    if with_square:
        square = own_ref[:, 2 * padded : 2 * padded + 1] + get_sums(arrived_ref, 2 * padded)
    return gate, up, square


def expand_first_kernel(cut, group_ref, gain_ref, gate_ref, up_ref, *refs):
    parts, (middle_ref, scaled_ref, own_ref, out_ref) = refs[:-4], refs[-4:]
    middle = parts[0][...].astype(F32)
    for part in parts[1:]:
        middle = middle + part[...].astype(F32)
    slots = middle_ref.shape[0]
    row = lax.broadcasted_iota(jnp.int32, (middle.shape[0], 1), 0)
    for slot in range(slots):
        own = jnp.where(row == group_ref[0] * slots + slot, middle, 0.0)
        middle_ref[slot : slot + 1] = jnp.sum(own, axis=0, keepdims=True)
    scaled = (middle * gain_ref[...].astype(F32)).astype(BF16)
    scaled_ref[...] = scaled
    put_terms(
        own_ref,
        out_ref,
        jnp.dot(scaled, gate_ref[:, :cut], preferred_element_type=F32),
        jnp.dot(scaled, up_ref[:, :cut], preferred_element_type=F32),
        jnp.sum(middle * middle, axis=1, keepdims=True),
    )


def expand_second_kernel(cut, scaled_ref, gate_ref, up_ref, own_ref, out_ref):
    scaled = scaled_ref[...]
    put_terms(
        own_ref,
        out_ref,
        jnp.dot(scaled, gate_ref[:, cut:], preferred_element_type=F32),
        jnp.dot(scaled, up_ref[:, cut:], preferred_element_type=F32),
        None,
    )


def merge_kernel(columns, with_square, first_ref, second_ref, own_ref, out_ref):
    put_terms(own_ref, out_ref, *get_terms(columns, first_ref, second_ref, with_square))


def activated(gate, up, factor):
    gate = gate * factor
    return (gate / (1.0 + jnp.exp(-gate)) * (up * factor)).astype(BF16)


def contracted(gate, up, factor, weight_ref, first):
    total = 0.0
    for start in range(0, gate.shape[1], CHUNK):
        part = slice(start, min(start + CHUNK, gate.shape[1]))
        total = total + jnp.dot(
            activated(gate[:, part], up[:, part], factor),
            weight_ref[first + part.start : first + part.stop, :],
            preferred_element_type=F32,
        )
    return total


def contract_first_kernel(cut, own_ref, arrived_ref, weight_ref, factor_ref, out_ref):
    gate, up, square = get_terms(cut, own_ref, arrived_ref, True)
    factor = lax.rsqrt(square / D + 1e-06)
    factor_ref[...] = jnp.broadcast_to(factor, factor_ref.shape)
    out_ref[...] = contracted(gate, up, factor, weight_ref, 0)


def contract_second_kernel(
    cut, own_ref, arrived_ref, weight_ref, factor_ref, partial_ref, out_ref
):
    gate, up, _ = get_terms(weight_ref.shape[0] - cut, own_ref, arrived_ref, False)
    total = partial_ref[...] + contracted(gate, up, factor_ref[:, :1], weight_ref, cut)
    slots = out_ref.shape[1]
    for owner in range(out_ref.shape[0]):
        out_ref[owner] = total[owner * slots : (owner + 1) * slots].astype(out_ref.dtype)


def exchange(array, first, second, wide, narrow):
    pairs = [
        (w * narrow + n, (w ^ (second if n % 2 else first)) * narrow + n)
        for w in range(wide)
        for n in range(narrow)
    ]
    return lax.ppermute(array, ("wide", "narrow"), pairs)


def exchange_groups(size):
    bits = size.bit_length() - 1
    groups = [[1]] if bits else []
    for bit in range(1, bits, 2):
        groups.append([part << bit for part in range(1, 4 if bit + 1 < bits else 2)])
    return groups


def swap(array, axis, distance, size):
    return lax.ppermute(array, axis, [(i, i ^ distance) for i in range(size)])


def shards(
    wide,
    narrow,
    residual_in,
    query_nope,
    query_rope,
    absorb_key,
    absorb_value,
    latent_cache,
    cache_lengths,
    slot_rows,
    out_proj,
    norm_gain,
    gate_weight,
    up_weight,
    down_weight,
):
    slots, heads, head_size = query_nope.shape
    rope = query_rope.shape[2]
    features = out_proj.shape[1]
    rows = slot_rows.shape[0]
    per_block = out_proj.shape[0] // head_size
    blocks = heads // per_block
    group = lax.axis_index("wide").astype(jnp.int32)
    scale = 1.0 / math.sqrt(head_size + rope)

    packed = call(
        pack_kernel,
        pltpu.VMEM((wide, slots, heads + heads // 2, head_size), BF16),
        [SMEM, HBM, HBM],
        "pack",
        [
            pltpu.VMEM(query_nope.shape, BF16),
            pltpu.VMEM(query_rope.shape, BF16),
            pltpu.SemaphoreType.DMA((2,)),
        ],
        flops=PACK,
    )(group[None], far(query_nope), far(query_rope))
    queries = lax.all_to_all(packed, "wide", 0, 0, tiled=True)
    cache = jnp.swapaxes(latent_cache, 1, 2)
    heads_out, select, spread = call(
        functools.partial(attend_kernel, narrow, blocks, scale),
        (
            pltpu.VMEM((wide * narrow, slots * per_block, head_size), BF16),
            pltpu.VMEM((rows * per_block, rows * per_block), BF16),
            pltpu.VMEM((rows, features), F32),
        ),
        [SMEM, SMEM, SMEM] + [VMEM] * 5,
        "attend",
        flops=ATTEND,
    )(
        group[None],
        slot_rows,
        cache_lengths,
        queries,
        near(absorb_key),
        near(cache),
        near(absorb_value),
        residual_in,
    )
    received = lax.all_to_all(heads_out, ("wide", "narrow"), 0, 0, tiled=True)
    total, summed = call(
        functools.partial(project_kernel, narrow, blocks),
        (pltpu.VMEM((rows, features), F32), pltpu.VMEM((rows, features), BF16)),
        [SMEM] + [VMEM] * 4,
        "project",
        flops=PROJECT,
    )(group[None], received, select, spread, out_proj)
    groups = exchange_groups(wide)
    for index, distances in enumerate(groups):
        others = [
            exchange(summed, first, second, wide, narrow)
            for first, second in zip(distances, distances[::-1])
        ]
        if index + 1 < len(groups):
            for other in others:
                total = total + other.astype(F32)
            summed = total.astype(BF16)
    columns = gate_weight.shape[1]
    cut = -(-2 * columns // 768) * 256
    halves = [(cut, 128, 256), (columns - cut, 0, 0)]
    shapes = []
    for size, kept, sent in halves:
        width = -(-size // 128) * 256
        shapes.append((pltpu.VMEM((rows, width + kept), F32), pltpu.VMEM((rows, width + sent), BF16)))
    middle, scaled, own, terms = call(
        functools.partial(expand_first_kernel, cut),
        (pltpu.VMEM((slots, features), F32), pltpu.VMEM((rows, features), BF16)) + shapes[0],
        [SMEM] + [VMEM] * (4 + len(others)),
        "expand_first",
        flops=EXPAND // 2,
    )(group[None], norm_gain[None, :], gate_weight, up_weight, total, *others)
    first = (own, terms)
    second = call(
        functools.partial(expand_second_kernel, cut),
        shapes[1],
        [VMEM] * 3,
        "expand_second",
        flops=EXPAND // 2,
    )(scaled, gate_weight, up_weight)
    distance = narrow // 2
    while distance:
        arrived = [swap(half[1], "narrow", distance, narrow) for half in (first, second)]
        distance //= 2
        if distance:
            first, second = (
                call(
                    functools.partial(merge_kernel, size, kept > 0),
                    shape,
                    [VMEM] * 2,
                    "merge",
                    flops=MERGE // 4,
                )(half[0], other)
                for (size, kept, _), shape, half, other in zip(
                    halves, shapes, (first, second), arrived
                )
            )
    factor, partial = call(
        functools.partial(contract_first_kernel, cut),
        (pltpu.VMEM((rows, 128), F32), pltpu.VMEM((rows, features), F32)),
        [VMEM] * 3,
        "contract_first",
        flops=CONTRACT // 4,
    )(first[0], arrived[0], down_weight)
    down = call(
        functools.partial(contract_second_kernel, cut),
        pltpu.VMEM((wide, slots, features), BF16),
        [VMEM] * 5,
        "contract_second",
        flops=CONTRACT,
    )(second[0], arrived[1], down_weight, factor, partial)
    total = jnp.sum(lax.all_to_all(down, "wide", 0, 0, tiled=True).astype(F32), axis=0)
    return (middle + total).astype(BF16)


def solution(mesh):
    in_specs = (
        P("wide", "narrow"),
        P("wide", "narrow", None),
        P("wide", "narrow", None),
        P("narrow", None, None),
        P("narrow", None, None),
        P("wide", None, None),
        P("wide"),
        P(),
        P("wide", "narrow"),
        P("narrow"),
        P("narrow", "wide"),
        P("narrow", "wide"),
        P("wide", "narrow"),
    )
    out_specs = P("wide", "narrow")
    body = functools.partial(shards, mesh.shape["wide"], mesh.shape["narrow"])
    return jax.shard_map(body, mesh=mesh, in_specs=in_specs, out_specs=out_specs, check_vma=False)
```
